32 devices in a mesh: gx: 4 (over y, core), gy: 2 (over x), gz: 4 (over z).
Axes of the slice: x: 2, y: 2, z: 4, core: 2. Of those that a mesh axis runs over, the one named last changes fastest.
Arguments:
- fields: float32 [5, 64, 64, 256], P(None, 'gz', 'gx', 'gy'), may hold values from -6 to 6
- tile_writer: int32 [4, 2, 320, 1], P('gx', 'gy', 'gz'), may hold values from 0 to 7; in each aligned block of 80 rows (0 to 79, 80 to 159, ..., all dimensions but the last counted through in order) at most 15 rows name the same one
Outputs:
- coarse_bands: float32 [5, 8, 8, 32], P(None, None, 'gx', 'gy')
- received: float32 [960, 8192], P(('gx', 'gy'), 'gz')
The draws below stay inside these ranges and needn't reach their ends.
Inputs may be any that keep to these rules, and one draw needn't show every extreme that they name: `tile_writer`: within each device's 80 entries, no destination is named more than 15 times, a bound that some block reaches.
All inputs are finite; a program needn't handle non-finite values.
Results may differ from the reference program's by a relative error of at most 0.00014.
Values sent between devices are 32-bit elements; how exact they have to be, the bound alone decides.
A program may use at most 64 MiB of HBM per device.

```python
import math
import jax
import jax.numpy as jnp
import numpy as np
from jax import lax

F = 5
BX = 16
BY = 128
BZ = 16
NX = 64
NY = 256
NZ = 64
TILES = 80
TILE = 2048
MOST = 15
N_GX = 4
N_GY = 2
N_GZ = 4


def block_scale(rng, extent, split, least, top_value):
    factor_of, own = 1.0, jax.random.fold_in(rng, 6)
    for dim, blocks in split:
        draws = jnp.exp(jax.random.uniform(jax.random.fold_in(own, dim), (blocks,), jnp.float32, least / len(split), top_value / len(split)))
        factor_of = factor_of * jnp.repeat(draws, extent[dim] // blocks).reshape([-1 if axis == dim else 1 for axis in range(len(extent))])
    return factor_of


def routed_block(key, own, number, rows, count, top, reach, lean):
    ranking = jax.random.permutation(key, count)
    crowded, usual = portions_of(count, rows * top, reach, lean, True), portions_of(count, rows * top, reach, lean, False)
    places = jnp.arange(count)

    def named(tallies, turn):
        used = int((tallies > 0).sum())
        fixed = max(1, used // 4)
        passed = fixed + (places - fixed + turn * (used - fixed)) % max(1, count - fixed)
        return jnp.zeros((count,), jnp.int32).at[ranking[jnp.where(places < fixed, places, passed)]].set(jnp.asarray(tallies, jnp.int32))

    tallies = jnp.where(number % 4 == 0, named(crowded, number // 4), named(usual, number - number // 4 - 1))
    mixed = jax.random.permutation(jax.random.fold_in(own, 3), count)
    giver, sink = mixed[0:count // 2 * 2:2], mixed[1:count // 2 * 2:2]
    slack = jnp.minimum(tallies[giver] - 1, reach - tallies[sink]) // 2
    slack = jnp.where((giver == ranking[0]) | (sink == ranking[0]) | (tallies[sink] == 0), 0, jnp.maximum(slack, 0))
    passed = jax.random.randint(jax.random.fold_in(own, 4), (count // 2,), 0, 1 << 20) % (slack + 1)
    tallies = tallies.at[giver].add(-passed).at[sink].add(passed)
    members = jnp.searchsorted(jnp.cumsum(tallies), jnp.arange(rows * top), side="right").astype(jnp.int32)
    grid = members.reshape(top, rows).T
    grid = grid[jax.random.permutation(jax.random.fold_in(own, 1), rows)]
    turn = jax.random.randint(jax.random.fold_in(own, 2), (rows, 1), 0, top)
    return jnp.take_along_axis(grid, (jnp.arange(top)[None, :] + turn) % top, axis=1)


def portions_of(number_of, total, most, lean, full):
    portions = [(1 << 20) // math.isqrt(grade ** lean) + 1 for grade in range(1, number_of + 1)]
    largest = most if full else min(most, max(-(-total // number_of), total * portions[0] // sum(portions)))
    least = 1 if total - largest >= number_of - 1 else 0
    counts, spare = [largest] + [least] * (number_of - 1), total - largest - least * (number_of - 1)
    while spare > 0:
        movable = [i for i in range(1, number_of) if counts[i] < largest] or [i for i in range(1, number_of) if counts[i] < most]
        whole, left = sum([portions[i] for i in movable]), spare
        for i in movable:
            extra = min(most - counts[i], max(1, left * portions[i] // whole), spare)
            counts[i] = counts[i] + extra
            spare = spare - extra
    return np.array(counts)


def bell_draw(stream_key, shape, width, bound, cuts=(), held_as=jnp.bfloat16):
    values = jax.random.normal(stream_key, shape, jnp.float32) * width
    if len(cuts) > 0:
        values = block_scale(stream_key, shape, cuts, -0.22, 0.18) * values
    return jnp.clip(values, min=-bound, max=bound).astype(held_as)


def setup_inputs(seed: int = 0) -> dict:
    arg_keys = jax.random.split(jax.random.key(seed), 3)
    fields = bell_draw(arg_keys[0], (F, NZ, NX, NY), 1.0, 6.0, ((1, 4), (2, 4), (3, 2)), jnp.float32)
    tile_writer_keys = jax.random.split(jax.random.fold_in(arg_keys[1], 1), N_GX * N_GY * (N_GZ * TILES) // TILES)
    tile_writer_turns = jax.random.permutation(jax.random.fold_in(arg_keys[1], 3), N_GX * N_GY * (N_GZ * TILES) // TILES)
    tile_writer = jax.vmap(lambda own, number: routed_block(jax.random.fold_in(arg_keys[1], 2), own, number, TILES, N_GX * N_GY, 1, MOST, 2))(tile_writer_keys, tile_writer_turns).reshape((N_GX, N_GY, N_GZ * TILES, 1))
    return {"fields": fields, "tile_writer": tile_writer}


PREDICT_ONE = -1.586134342059924
UPDATE_ONE = -0.052980118572961
PREDICT_TWO = 0.882911075530934
UPDATE_TWO = 0.443506852043971
LOW_SCALE = 1.0 / 1.149604398860241
HIGH_SCALE = 1.149604398860241


def lifting(values, along):
    length = values.shape[along]
    low_band = lax.slice_in_dim(values, 0, length, 2, along)
    high_band = lax.slice_in_dim(values, 1, length, 2, along)
    high_band = high_band + PREDICT_ONE * (low_band + jnp.roll(low_band, -1, along))
    low_band = low_band + UPDATE_ONE * (jnp.roll(high_band, 1, along) + high_band)
    high_band = high_band + PREDICT_TWO * (low_band + jnp.roll(low_band, -1, along))
    low_band = low_band + UPDATE_TWO * (jnp.roll(high_band, 1, along) + high_band)
    low_band = low_band * LOW_SCALE
    high_band = high_band * HIGH_SCALE
    joined = jnp.stack([low_band, high_band], axis=along + 1)
    return joined.reshape(values.shape)


def one_field(volume):
    results = []
    current = volume
    for depth in range(3):
        result = lifting(lifting(lifting(current, 1), 2), 0)
        results.append(result)
        current = result[::2, ::2, ::2]
    merged = results[2]
    for depth in (1, 0):
        merged = results[depth].at[::2, ::2, ::2].set(merged)
    return merged, current


def reference(fields, tile_writer):
    coefficients, coarse_three = lax.map(one_field, fields)
    level_four = lifting(coarse_three, 1)
    level_five = lifting(level_four[:, ::2], 1)
    coarse_bands = level_four.at[:, ::2].set(level_five)

    groups = N_GX * N_GY
    blocks = coefficients.reshape(F, N_GZ, BZ, N_GX, BX, N_GY, BY)
    blocks = blocks.transpose(3, 5, 1, 0, 2, 4, 6).reshape(groups, N_GZ, TILES, TILE)
    writers = tile_writer.reshape(groups, N_GZ, TILES).astype(jnp.int32)
    onehot = (writers[..., None] == jnp.arange(groups, dtype=jnp.int32)).astype(jnp.int32)
    slots = jnp.sum((jnp.cumsum(onehot, axis=2) - onehot) * onehot, axis=3).astype(jnp.int32)
    source = jnp.broadcast_to(jnp.arange(groups, dtype=jnp.int32)[:, None, None], writers.shape)
    layer = jnp.broadcast_to(jnp.arange(N_GZ, dtype=jnp.int32)[None, :, None], writers.shape)
    inbox = jnp.zeros((groups, groups * MOST, N_GZ, TILE), jnp.float32)
    inbox = inbox.at[writers, source * MOST + slots, layer].set(blocks)
    received = inbox.reshape(groups * groups * MOST, N_GZ * TILE)
    return coarse_bands, received
```

```python
import functools

import jax
import jax.numpy as jnp
from jax import lax
from jax.experimental import pallas as pl
from jax.experimental.pallas import tpu as pltpu
from jax.sharding import PartitionSpec as P

P1 = -1.586134342059924
U1 = -0.052980118572961
P2 = 0.882911075530934
U2 = 0.443506852043971
LOW = 1.0 / 1.149604398860241
HIGH = 1.149604398860241
LEVELS = 3


def coefficients(axis, step, row, lane):
    pos, other = (row, lane) if axis == 0 else (lane, row)
    active = other % step == 0
    high = active & (pos % (2 * step) == step)
    low = active & (pos % (2 * step) == 0)
    one = lambda where, value: jnp.where(where, jnp.float32(value), jnp.float32(0.0))
    scale = jnp.where(high, jnp.float32(HIGH), jnp.where(low, jnp.float32(LOW), jnp.float32(1.0)))
    return one(high, P1), one(low, U1), one(high, P2), one(low, U2), scale


def lift_in_place(v, axis, step, a, b, c, e, coefs, first, last):
    size = v.shape[axis]
    down = lambda u: pltpu.roll(u, step, axis)
    up = lambda u: pltpu.roll(u, size - step, axis)
    cp1, cu1, cp2, cu2, scale = coefs
    v1 = v + cp1 * (down(v) + jnp.where(last, c, up(v)))
    dm = a + P1 * v
    v2 = v1 + cu1 * (jnp.where(first, dm, down(v1)) + up(v1))
    sm = b + U1 * dm
    sp = e + U1 * v2
    v3 = v2 + cp2 * (down(v2) + jnp.where(last, sp, up(v2)))
    dm2 = dm + P2 * (sm + v2)
    v4 = v3 + cu2 * (jnp.where(first, dm2, down(v3)) + up(v3))
    return v4 * scale


def edge_sums(get, n):
    a = get(n - 1) + P1 * get(n - 2)
    before = get(n - 3) + P1 * (get(n - 4) + get(n - 2))
    b = get(n - 2) + U1 * before
    c = get(0)
    after = get(1) + P1 * (c + get(2))
    e = c + U1 * after
    return (a, b), (c, e)


def lift_layers(v, a, b, c, e):
    s, d = list(v[0::2]), list(v[1::2])
    n = len(s)
    s_end = [c]
    d = [d[i] + P1 * (s[i] + (s + s_end)[i + 1]) for i in range(n)]
    dm = a + P1 * s[0]
    sm = b + U1 * dm
    s_top = e + U1 * d[-1]
    s = [s[i] + U1 * (([dm] + d)[i] + d[i]) for i in range(n)]
    d = [d[i] + P2 * (s[i] + (s + [s_top])[i + 1]) for i in range(n)]
    dm = dm + P2 * (sm + s[0])
    s = [s[i] + U2 * (([dm] + d)[i] + d[i]) for i in range(n)]
    out = []
    for i in range(n):
        out += [s[i] * LOW, d[i] * HIGH]
    return out


def lift_whole(v):
    s, d = list(v[0::2]), list(v[1::2])
    n = len(s)
    d = [d[i] + P1 * (s[i] + s[(i + 1) % n]) for i in range(n)]
    s = [s[i] + U1 * (d[i - 1] + d[i]) for i in range(n)]
    d = [d[i] + P2 * (s[i] + s[(i + 1) % n]) for i in range(n)]
    s = [s[i] + U2 * (d[i - 1] + d[i]) for i in range(n)]
    out = []
    for i in range(n):
        out += [s[i] * LOW, d[i] * HIGH]
    return out


def kernel(sizes, source_ref, fields_ref, coarse_ref, inbox_ref, work, outbox, *scratch):
    n_gx, n_gy, n_gz, n_f, bz, capacity = sizes
    xs, xr, ys, yr, zs, zr = [scratch[LEVELS * i:LEVELS * (i + 1)] for i in range(6)]
    gs, gr, send, recv, g_send, g_recv, a_send, a_recv, own_sem = scratch[6 * LEVELS:]
    groups = n_gx * n_gy
    ix, iy, iz = lax.axis_index("gx"), lax.axis_index("gy"), lax.axis_index("gz")
    me = ix * n_gy + iy
    place = {"gx": (ix, n_gx), "gy": (iy, n_gy), "gz": (iz, n_gz)}

    barrier = pltpu.get_barrier_semaphore()

    def greet_plane(k, carry):
        w = lax.rem(me + k, groups)
        pl.semaphore_signal(barrier, inc=1, device_id={"gx": w // n_gy, "gy": lax.rem(w, n_gy)},
                            device_id_type=pl.DeviceIdType.MESH)
        return carry

    lax.fori_loop(1, groups, greet_plane, 0)
    for k in range(1, n_gz):
        pl.semaphore_signal(barrier, inc=1, device_id={"gz": lax.rem(iz + k, n_gz)},
                            device_id_type=pl.DeviceIdType.MESH)
    pl.semaphore_wait(barrier, groups - 1 + n_gz - 1)

    def exchange(level, kind, f, way):
        axis = ("gx", "gy", "gz")[kind]
        index, count = place[axis]
        target = lax.rem(index + (1 if way == 0 else count - 1), count)
        out, into = ((xs, xr), (ys, yr), (zs, zr))[kind]
        src = out[level].at[f] if kind == 1 else out[level].at[way, f]
        row = level * 3 + kind
        return pltpu.make_async_remote_copy(
            src_ref=src, dst_ref=into[level].at[way, f],
            send_sem=send.at[row, way, f], recv_sem=recv.at[row, way, f],
            device_id={axis: target}, device_id_type=pl.DeviceIdType.MESH)

    row = lax.broadcasted_iota(jnp.int32, (16, 128), 0)
    lane = lax.broadcasted_iota(jnp.int32, (16, 128), 1)

    def send_x(level, f, tiles):
        step = 1 << level
        for i, tile in enumerate(tiles):
            get = lambda k: tile[k * step:k * step + 1, :]
            for way, pair in enumerate(edge_sums(get, 16 // step)):
                for j in range(2):
                    xs[level][way, f, i, j:j + 1, :] = pair[j]
        for way in range(2):
            exchange(level, 0, f, way).start()

    def send_y(level, f, tiles):
        step = 1 << level
        pack = jnp.zeros((16, 128), jnp.float32)
        for i, v in enumerate(tiles):
            r1, r2 = pltpu.roll(v, step, 1), pltpu.roll(v, 128 - step, 1)
            t = U1 * (v + P1 * (r1 + r2))
            c = jnp.where(lane == 0, v, jnp.where(lane == step, r1 + t, jnp.where(
                lane == 128 - 3 * step, r2 + t, v + P1 * r1)))
            at = i * 8 * step
            moved = pltpu.roll(c, (at + 3 * step) % 128, 1)
            pack = jnp.where((lane >= at) & (lane < at + 8 * step), moved, pack)
        ys[level][f] = pack
        for way in range(2):
            exchange(level, 1, f, way).start()

    def send_z(level, f, tiles):
        for way, pair in enumerate(edge_sums(lambda k: tiles[k], len(tiles))):
            for j in range(2):
                zs[level][way, f, j] = pair[j]
        for way in range(2):
            exchange(level, 2, f, way).start()

    def planes(f, step, ref):
        return [ref[f * bz + z] if ref is work else ref[f, z] for z in range(0, bz, step)]

    def put(f, step, tiles):
        for i, tile in enumerate(tiles):
            work[f * bz + i * step] = tile

    def loop(body):
        def run(f, carry):
            body(f)
            return carry
        lax.fori_loop(0, n_f, run, 0)

    loop(lambda f: send_x(0, f, planes(f, 1, fields_ref)))
    for level in range(LEVELS):
        step = 1 << level

        def x_stage(f, level=level, step=step):
            coefs = coefficients(0, step, row, lane)
            tiles = planes(f, step, fields_ref if level == 0 else work)
            for way in range(2):
                exchange(level, 0, f, way).wait_recv()
            done = []
            for i, v in enumerate(tiles):
                a, b = [xr[level][0, f, i, j:j + 1, :] for j in range(2)]
                c, e = [xr[level][1, f, i, j:j + 1, :] for j in range(2)]
                done.append(lift_in_place(v, 0, step, a, b, c, e, coefs, row == 0, row == 16 - step))
            put(f, step, done)
            send_y(level, f, done)

        loop(x_stage)

        def y_stage(f, level=level, step=step):
            coefs = coefficients(1, step, row, lane)
            for way in range(2):
                exchange(level, 1, f, way).wait_recv()
            below, above = yr[level][0, f], yr[level][1, f]
            done = []
            for i, v in enumerate(planes(f, step, work)):
                at = i * 8 * step
                turn = lambda u, k: pltpu.roll(u, k % 128, 1) if k % 128 else u
                a, b = turn(below, -at - 2 * step), turn(below, -at)
                c, e = turn(above, -at - 4 * step), turn(above, -at - 5 * step)
                done.append(lift_in_place(v, 1, step, a, b, c, e, coefs, lane == 0, lane == 128 - step))
            put(f, step, done)
            send_z(level, f, done)

        loop(y_stage)

        def z_stage(f, level=level, step=step):
            old = planes(f, step, work)
            for way in range(2):
                exchange(level, 2, f, way).wait_recv()
            a, b = zr[level][0, f, 0], zr[level][0, f, 1]
            c, e = zr[level][1, f, 0], zr[level][1, f, 1]
            new = lift_layers(old, a, b, c, e)
            if step > 1:
                live = (row % step == 0) & (lane % step == 0)
                new = [jnp.where(live, n, o) for n, o in zip(new, old)]
            put(f, step, new)
            if level + 1 < LEVELS:
                send_x(level + 1, f, new[::2])
            else:
                for i, tile in enumerate(new[::2]):
                    for j in range(2):
                        gs[f, i, j:j + 1, :] = tile[8 * j:8 * j + 1, :]

        loop(z_stage)

    def gather(k):
        return pltpu.make_async_remote_copy(
            src_ref=gs, dst_ref=gr.at[iz], send_sem=g_send.at[k], recv_sem=g_recv.at[k],
            device_id={"gz": lax.rem(iz + k, n_gz)}, device_id_type=pl.DeviceIdType.MESH)

    for k in range(1, n_gz):
        gather(k).start()
    gr[iz] = gs[...]

    work[n_f * bz] = jnp.zeros((16, 128), jnp.float32)

    def route(k):
        w = lax.rem(me + k, groups)
        return pltpu.make_async_remote_copy(
            src_ref=outbox.at[w], dst_ref=inbox_ref.at[me], send_sem=a_send.at[k], recv_sem=a_recv.at[k],
            device_id={"gx": w // n_gy, "gy": lax.rem(w, n_gy)}, device_id_type=pl.DeviceIdType.MESH)

    def pack(w):
        for r in range(capacity):
            outbox[w, r] = work[source_ref[w * capacity + r]]

    def pack_and_send(k, carry):
        pack(lax.rem(me + k, groups))
        route(k).start()
        return carry

    lax.fori_loop(1, groups, pack_and_send, 0)
    pack(me)
    own = pltpu.make_async_copy(outbox.at[me], inbox_ref.at[me], own_sem)
    own.start()

    for k in range(1, n_gz):
        gather(k).wait_recv()
    for f in range(n_f):
        column = [gr[g, f, i] for g in range(n_gz) for i in range(2)]
        four = lift_whole(column)
        four[::2] = lift_whole(four[::2])
        for z, tile in enumerate(four):
            coarse_ref[f, z] = tile

    def finish(k, carry):
        route(k).wait()
        return carry

    lax.fori_loop(1, groups, finish, 0)
    own.wait()
    for k in range(1, n_gz):
        gather(k).wait_send()

    def sent(f):
        for level in range(LEVELS):
            for kind in range(3):
                for way in range(2):
                    exchange(level, kind, f, way).wait_send()

    loop(sent)


def source_table(writers, groups, capacity):
    count = writers.shape[0]
    place = jnp.arange(count, dtype=jnp.int32)
    same = (writers[:, None] == writers[None, :]) & (place[None, :] < place[:, None])
    targets = writers * capacity + jnp.sum(same.astype(jnp.int32), axis=1)
    slots = jnp.arange(groups * capacity, dtype=jnp.int32)
    hit = (targets[None, :] == slots[:, None]).astype(jnp.int32)
    return count - jnp.sum(hit * (count - place)[None, :], axis=1)


def body(fields, tile_writer):
    n_gx, n_gy, n_gz = lax.axis_size("gx"), lax.axis_size("gy"), lax.axis_size("gz")
    n_f, bz, bx, by = fields.shape
    count = n_f * bz
    groups = n_gx * n_gy
    capacity = max(2, 7 * count // (5 * groups) + 1)
    source = source_table(tile_writer.reshape(count), groups, capacity)
    f32 = jnp.float32
    steps = [1 << level for level in range(LEVELS)]
    scratch = [pltpu.VMEM((count + 1, bx, by), f32), pltpu.VMEM((groups, capacity, bx, by), f32)]
    scratch += [pltpu.VMEM((2, n_f, bz // s, 2, by), f32) for s in steps] * 2
    scratch += [pltpu.VMEM((n_f, bx, by), f32) for s in steps]
    scratch += [pltpu.VMEM((2, n_f, bx, by), f32) for s in steps]
    scratch += [pltpu.VMEM((2, n_f, 2, bx, by), f32) for s in steps] * 2
    scratch += [pltpu.VMEM((n_f, 2, 2, by), f32), pltpu.VMEM((n_gz, n_f, 2, 2, by), f32)]
    scratch += [pltpu.SemaphoreType.DMA((3 * LEVELS, 2, n_f))] * 2
    scratch += [pltpu.SemaphoreType.DMA((n_gz,))] * 2 + [pltpu.SemaphoreType.DMA((groups,))] * 2
    scratch += [pltpu.SemaphoreType.DMA]
    coarse, inbox = pl.pallas_call(
        functools.partial(kernel, (n_gx, n_gy, n_gz, n_f, bz, capacity)),
        out_shape=(jax.ShapeDtypeStruct((n_f, 2 * n_gz, 2, by), f32),
                   jax.ShapeDtypeStruct((groups, capacity, bx, by), f32)),
        in_specs=[pl.BlockSpec(memory_space=pltpu.SMEM), pl.BlockSpec(memory_space=pltpu.VMEM)],
        out_specs=(pl.BlockSpec(memory_space=pltpu.VMEM), pl.BlockSpec(memory_space=pl.ANY)),
        scratch_shapes=scratch,
        compiler_params=pltpu.CompilerParams(collective_id=0, has_side_effects=True,
                                             vmem_limit_bytes=32 * 1024 * 1024),
    )(source, fields)
    return coarse[..., ::8], inbox.reshape(groups * capacity, bx * by)


def solution(mesh):
    return jax.shard_map(
        body,
        mesh=mesh,
        in_specs=(P(None, "gz", "gx", "gy"), P("gx", "gy", "gz", None)),
        out_specs=(P(None, None, "gx", "gy"), P(("gx", "gy"), "gz")),
        check_vma=False,
    )
```

```python
import functools

import jax
import jax.numpy as jnp
from jax import lax
from jax.experimental import pallas as pl
from jax.experimental.pallas import tpu as pltpu
from jax.sharding import PartitionSpec as P

P1 = -1.586134342059924
U1 = -0.052980118572961
P2 = 0.882911075530934
U2 = 0.443506852043971
LOW = 1.0 / 1.149604398860241
HIGH = 1.149604398860241
LEVELS = 3


def coefficients(axis, step, row, lane):
    pos, other = (row, lane) if axis == 0 else (lane, row)
    active = other % step == 0
    high = active & (pos % (2 * step) == step)
    low = active & (pos % (2 * step) == 0)
    one = lambda where, value: jnp.where(where, jnp.float32(value), jnp.float32(0.0))
    scale = jnp.where(high, jnp.float32(HIGH), jnp.where(low, jnp.float32(LOW), jnp.float32(1.0)))
    return one(high, P1), one(low, U1), one(high, P2), one(low, U2), scale


def lift_in_place(v, axis, step, a, b, c, e, coefs, first, last):
    size = v.shape[axis]
    down = lambda u: pltpu.roll(u, step, axis)
    up = lambda u: pltpu.roll(u, size - step, axis)
    cp1, cu1, cp2, cu2, scale = coefs
    v1 = v + cp1 * (down(v) + jnp.where(last, c, up(v)))
    dm = a + P1 * v
    v2 = v1 + cu1 * (jnp.where(first, dm, down(v1)) + up(v1))
    sm = b + U1 * dm
    sp = e + U1 * v2
    v3 = v2 + cp2 * (down(v2) + jnp.where(last, sp, up(v2)))
    dm2 = dm + P2 * (sm + v2)
    v4 = v3 + cu2 * (jnp.where(first, dm2, down(v3)) + up(v3))
    return v4 * scale


def edge_sums(get, n):
    a = get(n - 1) + P1 * get(n - 2)
    before = get(n - 3) + P1 * (get(n - 4) + get(n - 2))
    b = get(n - 2) + U1 * before
    c = get(0)
    after = get(1) + P1 * (c + get(2))
    e = c + U1 * after
    return (a, b), (c, e)


def lift_layers(v, a, b, c, e):
    s, d = list(v[0::2]), list(v[1::2])
    n = len(s)
    s_end = [c]
    d = [d[i] + P1 * (s[i] + (s + s_end)[i + 1]) for i in range(n)]
    dm = a + P1 * s[0]
    sm = b + U1 * dm
    s_top = e + U1 * d[-1]
    s = [s[i] + U1 * (([dm] + d)[i] + d[i]) for i in range(n)]
    d = [d[i] + P2 * (s[i] + (s + [s_top])[i + 1]) for i in range(n)]
    dm = dm + P2 * (sm + s[0])
    s = [s[i] + U2 * (([dm] + d)[i] + d[i]) for i in range(n)]
    out = []
    for i in range(n):
        out += [s[i] * LOW, d[i] * HIGH]
    return out


def lift_whole(v):
    s, d = list(v[0::2]), list(v[1::2])
    n = len(s)
    d = [d[i] + P1 * (s[i] + s[(i + 1) % n]) for i in range(n)]
    s = [s[i] + U1 * (d[i - 1] + d[i]) for i in range(n)]
    d = [d[i] + P2 * (s[i] + s[(i + 1) % n]) for i in range(n)]
    s = [s[i] + U2 * (d[i - 1] + d[i]) for i in range(n)]
    out = []
    for i in range(n):
        out += [s[i] * LOW, d[i] * HIGH]
    return out


def kernel(sizes, source_ref, fields_ref, coarse_ref, received_ref, work, outbox, inbox, *scratch):
    n_gx, n_gy, n_gz, n_f, bz, capacity = sizes
    xs, xr, ys, yr, zs, zr, cs, cr = [scratch[LEVELS * i:LEVELS * (i + 1)] for i in range(8)]
    low_rows, gs, gr, send, recv, c_send, c_recv, g_send, g_recv, a_send, a_recv, own_sem = scratch[8 * LEVELS:]
    groups = n_gx * n_gy
    ix, iy, iz = lax.axis_index("gx"), lax.axis_index("gy"), lax.axis_index("gz")
    me = ix * n_gy + iy
    place = {"gx": (ix, n_gx), "gy": (iy, n_gy), "gz": (iz, n_gz)}
    MESH = pl.DeviceIdType.MESH

    def beside(axis, way):
        index, count = place[axis]
        return lax.rem(index + (1 if way == 0 else count - 1), count)

    barrier = pltpu.get_barrier_semaphore()

    def greet_plane(k, carry):
        w = lax.rem(me + k, groups)
        pl.semaphore_signal(barrier, inc=1, device_id={"gx": w // n_gy, "gy": lax.rem(w, n_gy)},
                            device_id_type=MESH)
        return carry

    lax.fori_loop(1, groups, greet_plane, 0)
    for k in range(1, n_gz):
        pl.semaphore_signal(barrier, inc=1, device_id={"gz": lax.rem(iz + k, n_gz)}, device_id_type=MESH)
    for yway in range(2):
        for zway in range(2):
            pl.semaphore_signal(barrier, inc=1, device_id={"gy": beside("gy", yway), "gz": beside("gz", zway)},
                                device_id_type=MESH)
    pl.semaphore_wait(barrier, groups - 1 + n_gz - 1 + 4)

    def exchange(level, kind, f, way):
        axis = ("gx", "gy", "gz")[kind]
        out, into = ((xs, xr), (ys, yr), (zs, zr))[kind]
        src = out[level].at[f] if kind == 1 else out[level].at[way, f]
        row = level * 3 + kind
        return pltpu.make_async_remote_copy(
            src_ref=src, dst_ref=into[level].at[way, f],
            send_sem=send.at[row, way, f], recv_sem=recv.at[row, way, f],
            device_id={axis: beside(axis, way)}, device_id_type=MESH)

    def corner(level, yway, zway):
        return pltpu.make_async_remote_copy(
            src_ref=cs[level].at[zway], dst_ref=cr[level].at[yway, zway],
            send_sem=c_send.at[level, yway, zway], recv_sem=c_recv.at[level, yway, zway],
            device_id={"gy": beside("gy", yway), "gz": beside("gz", zway)}, device_id_type=MESH)

    row = lax.broadcasted_iota(jnp.int32, (16, 128), 0)
    lane = lax.broadcasted_iota(jnp.int32, (16, 128), 1)

    def send_x(level, f, tiles):
        step = 1 << level
        for i, tile in enumerate(tiles):
            get = lambda k: tile[k * step:k * step + 1, :]
            for way, pair in enumerate(edge_sums(get, 16 // step)):
                for j in range(2):
                    xs[level][way, f, i, j:j + 1, :] = pair[j]
        for way in range(2):
            exchange(level, 0, f, way).start()

    def spot(i, step):
        return i // step * (8 * step) + i % step

    def packed(step, pairs, pack):
        for i, v in pairs:
            r1, r2 = pltpu.roll(v, step, 1), pltpu.roll(v, 128 - step, 1)
            t = U1 * (v + P1 * (r1 + r2))
            c = jnp.where(lane == 0, v, jnp.where(lane == step, r1 + t, jnp.where(
                lane == 128 - 3 * step, r2 + t, v + P1 * r1)))
            start = i // step * (8 * step)
            here = (lane >= start) & (lane < start + 8 * step) & (lane % step == i % step)
            pack = jnp.where(here, pltpu.roll(c, (spot(i, step) + 3 * step) % 128, 1), pack)
        return pack

    def y_lift(step, i, v, below, above):
        at = spot(i, step)
        def turn(u, k):
            k = (k + 256) % 128
            return u if isinstance(k, int) and k == 0 else pltpu.roll(u, k, 1)
        a, b = turn(below, -at - 2 * step), turn(below, -at)
        c, e = turn(above, -at - 4 * step), turn(above, -at - 5 * step)
        coefs = coefficients(1, step, row, lane)
        return lift_in_place(v, 1, step, a, b, c, e, coefs, lane == 0, lane == 128 - step)

    def planes(f, step, ref):
        return [ref[f * bz + z] if ref is work else ref[f, z] for z in range(0, bz, step)]

    def put(f, step, tiles):
        for i, tile in enumerate(tiles):
            work[f * bz + i * step] = tile

    def loop(body):
        def run(f, carry):
            body(f)
            return carry
        lax.fori_loop(0, n_f, run, 0)

    def route(part, k):
        w = lax.rem(me + k, groups)
        return pltpu.make_async_remote_copy(
            src_ref=outbox.at[part, w], dst_ref=inbox.at[part, pl.ds(me * (8 * capacity), 8 * capacity)],
            send_sem=a_send.at[part, k], recv_sem=a_recv.at[part, k],
            device_id={"gx": w // n_gy, "gy": lax.rem(w, n_gy)}, device_id_type=MESH)

    def own(part):
        return pltpu.make_async_copy(
            outbox.at[part, me], inbox.at[part, pl.ds(me * (8 * capacity), 8 * capacity)], own_sem.at[part])

    def fill(part, w):
        for r in range(capacity):
            outbox[part, w, 8 * r:8 * r + 8] = work[source_ref[w * capacity + r], pl.ds(part, 8, 2), :]

    def ship(part, first, last):
        def run(k, carry):
            fill(part, lax.rem(me + k, groups))
            route(part, k).start()
            return carry
        lax.fori_loop(first, last, run, 0)

    cuts = [1 + (groups - 1) * i // 4 for i in range(5)]
    work[n_f * bz] = jnp.zeros((16, 128), jnp.float32)
    loop(lambda f: send_x(0, f, planes(f, 1, fields_ref)))
    for level in range(LEVELS):
        step = 1 << level
        if level > 0:
            ship(1, cuts[2 * level - 2], cuts[2 * level - 1])
        for zway in range(2):
            cs[level][zway] = jnp.zeros((16, 128), jnp.float32)

        def x_stage(f, level=level, step=step):
            coefs = coefficients(0, step, row, lane)
            tiles = planes(f, step, fields_ref if level == 0 else work)
            for way in range(2):
                exchange(level, 0, f, way).wait_recv()
            done = []
            for i, v in enumerate(tiles):
                a, b = [xr[level][0, f, i, j:j + 1, :] for j in range(2)]
                c, e = [xr[level][1, f, i, j:j + 1, :] for j in range(2)]
                done.append(lift_in_place(v, 0, step, a, b, c, e, coefs, row == 0, row == 16 - step))
            put(f, step, done)
            sums = edge_sums(lambda k: done[k], len(done))
            for way in range(2):
                for j in range(2):
                    zs[level][way, f, j] = sums[way][j]
                exchange(level, 2, f, way).start()
            ys[level][f] = packed(step, list(enumerate(done)), jnp.zeros((16, 128), jnp.float32))
            for way in range(2):
                exchange(level, 1, f, way).start()
            for way in range(2):
                cs[level][way] = packed(step, [(2 * f + j, sums[way][j]) for j in range(2)], cs[level][way])

        loop(x_stage)
        for yway in range(2):
            for zway in range(2):
                corner(level, yway, zway).start()
        if level > 0:
            ship(1, cuts[2 * level - 1], cuts[2 * level])

        def y_stage(f, level=level, step=step):
            for way in range(2):
                exchange(level, 1, f, way).wait_recv()
            below, above = yr[level][0, f], yr[level][1, f]
            put(f, step, [y_lift(step, i, v, below, above) for i, v in enumerate(planes(f, step, work))])

        loop(y_stage)
        for yway in range(2):
            for zway in range(2):
                corner(level, yway, zway).wait_recv()

        def z_stage(f, level=level, step=step):
            old = planes(f, step, work)
            for way in range(2):
                exchange(level, 2, f, way).wait_recv()
            edge = [[y_lift(step, 2 * f + j, zr[level][way, f, j], cr[level][0, way], cr[level][1, way])
                     for j in range(2)] for way in range(2)]
            new = lift_layers(old, *edge[0], *edge[1])
            if step > 1:
                live = (row % step == 0) & (lane % step == 0)
                new = [jnp.where(live, n, o) for n, o in zip(new, old)]
            put(f, step, new)
            if level + 1 < LEVELS:
                send_x(level + 1, f, new[::2])

        loop(z_stage)

    def gather(k):
        return pltpu.make_async_remote_copy(
            src_ref=gs, dst_ref=gr.at[iz], send_sem=g_send.at[k], recv_sem=g_recv.at[k],
            device_id={"gz": lax.rem(iz + k, n_gz)}, device_id_type=MESH)

    for i in range(2):
        for f in range(n_f):
            for j in range(2):
                low_rows[16 * i + 2 * f + j:16 * i + 2 * f + j + 1, :] = work[f * bz + 8 * i, 8 * j:8 * j + 1, :]
        low_rows[16 * i + 2 * n_f:16 * i + 16, :] = jnp.zeros((16 - 2 * n_f, 128), jnp.float32)
    pick = jnp.where(lax.broadcasted_iota(jnp.int32, (128, 128), 0) ==
                     8 * lax.broadcasted_iota(jnp.int32, (128, 128), 1), jnp.float32(1.0), jnp.float32(0.0))
    gs[...] = jnp.dot(low_rows[...], pick, precision=lax.Precision.HIGHEST, preferred_element_type=jnp.float32)
    for k in range(1, n_gz):
        gather(k).start()
    gr[iz] = gs[...]

    ship(0, 1, groups)
    for part in range(2):
        fill(part, me)
        own(part).start()

    for k in range(1, n_gz):
        gather(k).wait_recv()
    four = lift_whole([gr[g, 16 * i:16 * i + 16, :] for g in range(n_gz) for i in range(2)])
    four[::2] = lift_whole(four[::2])
    for z, tile in enumerate(four):
        for f in range(n_f):
            coarse_ref[f, z] = tile[2 * f:2 * f + 2, :16]

    def finish(k, carry):
        for part in range(2):
            route(part, k).wait()
        return carry

    lax.fori_loop(1, groups, finish, 0)
    for part in range(2):
        own(part).wait()

    def unpack(k, carry):
        for part in range(2):
            for x in range(8):
                at = (2 * x + part) * 128
                received_ref[pl.ds(pl.multiple_of(8 * k, 8), 8), at:at + 128] = (
                    inbox[part, pl.ds(64 * k + x, 8, 8), :])
        return carry

    lax.fori_loop(0, groups * capacity // 8, unpack, 0)
    for k in range(1, n_gz):
        gather(k).wait_send()

    def sent(f):
        for level in range(LEVELS):
            for kind in range(3):
                for way in range(2):
                    exchange(level, kind, f, way).wait_send()

    loop(sent)
    for level in range(LEVELS):
        for yway in range(2):
            for zway in range(2):
                corner(level, yway, zway).wait_send()


def source_table(writers, groups, capacity):
    count = writers.shape[0]
    place = jnp.arange(count, dtype=jnp.int32)
    same = (writers[:, None] == writers[None, :]) & (place[None, :] < place[:, None])
    targets = writers * capacity + jnp.sum(same.astype(jnp.int32), axis=1)
    slots = jnp.arange(groups * capacity, dtype=jnp.int32)
    hit = (targets[None, :] == slots[:, None]).astype(jnp.int32)
    return count - jnp.sum(hit * (count - place)[None, :], axis=1)


def body(fields, tile_writer):
    n_gx, n_gy, n_gz = lax.axis_size("gx"), lax.axis_size("gy"), lax.axis_size("gz")
    n_f, bz, bx, by = fields.shape
    count = n_f * bz
    groups = n_gx * n_gy
    capacity = max(2, 7 * count // (5 * groups) + 1)
    source = source_table(tile_writer.reshape(count), groups, capacity)
    f32 = jnp.float32
    steps = [1 << level for level in range(LEVELS)]
    scratch = [pltpu.VMEM((count + 1, bx, by), f32), pltpu.VMEM((2, groups, 8 * capacity, by), f32),
               pltpu.VMEM((2, groups * 8 * capacity, by), f32)]
    scratch += [pltpu.VMEM((2, n_f, bz // s, 2, by), f32) for s in steps] * 2
    scratch += [pltpu.VMEM((n_f, bx, by), f32) for s in steps]
    scratch += [pltpu.VMEM((2, n_f, bx, by), f32) for s in steps]
    scratch += [pltpu.VMEM((2, n_f, 2, bx, by), f32) for s in steps] * 2
    scratch += [pltpu.VMEM((2, bx, by), f32) for s in steps] + [pltpu.VMEM((2, 2, bx, by), f32) for s in steps]
    scratch += [pltpu.VMEM((32, by), f32)] * 2 + [pltpu.VMEM((n_gz, 32, by), f32)]
    scratch += [pltpu.SemaphoreType.DMA((3 * LEVELS, 2, n_f))] * 2
    scratch += [pltpu.SemaphoreType.DMA((LEVELS, 2, 2))] * 2
    scratch += [pltpu.SemaphoreType.DMA((n_gz,))] * 2 + [pltpu.SemaphoreType.DMA((2, groups))] * 2
    scratch += [pltpu.SemaphoreType.DMA((2,))]
    return pl.pallas_call(
        functools.partial(kernel, (n_gx, n_gy, n_gz, n_f, bz, capacity)),
        out_shape=(jax.ShapeDtypeStruct((n_f, 2 * n_gz, 2, by // 8), f32),
                   jax.ShapeDtypeStruct((groups * capacity, bx * by), f32)),
        in_specs=[pl.BlockSpec(memory_space=pltpu.SMEM), pl.BlockSpec(memory_space=pltpu.VMEM)],
        out_specs=(pl.BlockSpec(memory_space=pltpu.VMEM), pl.BlockSpec(memory_space=pltpu.VMEM)),
        scratch_shapes=scratch,
        compiler_params=pltpu.CompilerParams(collective_id=0, has_side_effects=True,
                                             vmem_limit_bytes=32 * 1024 * 1024),
    )(source, fields)


def solution(mesh):
    return jax.shard_map(
        body,
        mesh=mesh,
        in_specs=(P(None, "gz", "gx", "gy"), P("gx", "gy", "gz", None)),
        out_specs=(P(None, None, "gx", "gy"), P(("gx", "gy"), "gz")),
        check_vma=False,
    )
```

```python
import functools

import jax
import jax.numpy as jnp
from jax import lax
from jax.experimental import pallas as pl
from jax.experimental.pallas import tpu as pltpu
from jax.sharding import PartitionSpec as P

P1 = -1.586134342059924
U1 = -0.052980118572961
P2 = 0.882911075530934
U2 = 0.443506852043971
LOW = 1.0 / 1.149604398860241
HIGH = 1.149604398860241
LEVELS = 3


def coefficients(axis, step, row, lane):
    pos, other = (row, lane) if axis == 0 else (lane, row)
    active = other % step == 0
    high = active & (pos % (2 * step) == step)
    low = active & (pos % (2 * step) == 0)
    one = lambda where, value: jnp.where(where, jnp.float32(value), jnp.float32(0.0))
    scale = jnp.where(high, jnp.float32(HIGH), jnp.where(low, jnp.float32(LOW), jnp.float32(1.0)))
    return one(high, P1), one(low, U1), one(high, P2), one(low, U2), scale


def lift_in_place(v, axis, step, a, b, c, e, coefs, first, last):
    size = v.shape[axis]
    down = lambda u: pltpu.roll(u, step, axis)
    up = lambda u: pltpu.roll(u, size - step, axis)
    cp1, cu1, cp2, cu2, scale = coefs
    v1 = v + cp1 * (down(v) + jnp.where(last, c, up(v)))
    dm = a + P1 * v
    v2 = v1 + cu1 * (jnp.where(first, dm, down(v1)) + up(v1))
    sm = b + U1 * dm
    sp = e + U1 * v2
    v3 = v2 + cp2 * (down(v2) + jnp.where(last, sp, up(v2)))
    dm2 = dm + P2 * (sm + v2)
    v4 = v3 + cu2 * (jnp.where(first, dm2, down(v3)) + up(v3))
    return v4 * scale


def edge_sums(get, n):
    a = get(n - 1) + P1 * get(n - 2)
    before = get(n - 3) + P1 * (get(n - 4) + get(n - 2))
    b = get(n - 2) + U1 * before
    c = get(0)
    after = get(1) + P1 * (c + get(2))
    e = c + U1 * after
    return (a, b), (c, e)


def lift_layers(v, a, b, c, e):
    s, d = list(v[0::2]), list(v[1::2])
    n = len(s)
    s_end = [c]
    d = [d[i] + P1 * (s[i] + (s + s_end)[i + 1]) for i in range(n)]
    dm = a + P1 * s[0]
    sm = b + U1 * dm
    s_top = e + U1 * d[-1]
    s = [s[i] + U1 * (([dm] + d)[i] + d[i]) for i in range(n)]
    d = [d[i] + P2 * (s[i] + (s + [s_top])[i + 1]) for i in range(n)]
    dm = dm + P2 * (sm + s[0])
    s = [s[i] + U2 * (([dm] + d)[i] + d[i]) for i in range(n)]
    out = []
    for i in range(n):
        out += [s[i] * LOW, d[i] * HIGH]
    return out


def lift_whole(v):
    s, d = list(v[0::2]), list(v[1::2])
    n = len(s)
    d = [d[i] + P1 * (s[i] + s[(i + 1) % n]) for i in range(n)]
    s = [s[i] + U1 * (d[i - 1] + d[i]) for i in range(n)]
    d = [d[i] + P2 * (s[i] + s[(i + 1) % n]) for i in range(n)]
    s = [s[i] + U2 * (d[i - 1] + d[i]) for i in range(n)]
    out = []
    for i in range(n):
        out += [s[i] * LOW, d[i] * HIGH]
    return out


def kernel(sizes, source_ref, fields_ref, coarse_ref, received_ref, work, outbox, inbox, *scratch):
    n_gx, n_gy, n_gz, n_f, bz, capacity = sizes
    xs, xr, ys, yr, zs, zr, cs, cr = [scratch[LEVELS * i:LEVELS * (i + 1)] for i in range(8)]
    low_rows, gs, gr, send, recv, c_send, c_recv, g_send, g_recv, a_send, a_recv, own_sem = scratch[8 * LEVELS:]
    groups = n_gx * n_gy
    ix, iy, iz = lax.axis_index("gx"), lax.axis_index("gy"), lax.axis_index("gz")
    me = ix * n_gy + iy
    place = {"gx": (ix, n_gx), "gy": (iy, n_gy), "gz": (iz, n_gz)}
    MESH = pl.DeviceIdType.MESH

    def beside(axis, way):
        index, count = place[axis]
        return lax.rem(index + (1 if way == 0 else count - 1), count)

    barrier = pltpu.get_barrier_semaphore()

    def greet_plane(k, carry):
        w = lax.rem(me + k, groups)
        pl.semaphore_signal(barrier, inc=1, device_id={"gx": w // n_gy, "gy": lax.rem(w, n_gy)},
                            device_id_type=MESH)
        return carry

    lax.fori_loop(1, groups, greet_plane, 0)
    for k in range(1, n_gz):
        pl.semaphore_signal(barrier, inc=1, device_id={"gz": lax.rem(iz + k, n_gz)}, device_id_type=MESH)
    for yway in range(2):
        for zway in range(2):
            pl.semaphore_signal(barrier, inc=1, device_id={"gy": beside("gy", yway), "gz": beside("gz", zway)},
                                device_id_type=MESH)
    pl.semaphore_wait(barrier, groups - 1 + n_gz - 1 + 4)

    def exchange(level, kind, f, way):
        axis = ("gx", "gy", "gz")[kind]
        out, into = ((xs, xr), (ys, yr), (zs, zr))[kind]
        src = out[level] if kind == 1 else out[level].at[way]
        dst = into[level].at[way]
        if level == 0:
            src, dst = src.at[f], dst.at[f]
        else:
            f = 0
        row = level * 3 + kind
        return pltpu.make_async_remote_copy(
            src_ref=src, dst_ref=dst,
            send_sem=send.at[row, way, f], recv_sem=recv.at[row, way, f],
            device_id={axis: beside(axis, way)}, device_id_type=MESH)

    def corner(level, yway, zway):
        return pltpu.make_async_remote_copy(
            src_ref=cs[level].at[zway], dst_ref=cr[level].at[yway, zway],
            send_sem=c_send.at[level, yway, zway], recv_sem=c_recv.at[level, yway, zway],
            device_id={"gy": beside("gy", yway), "gz": beside("gz", zway)}, device_id_type=MESH)

    row = lax.broadcasted_iota(jnp.int32, (16, 128), 0)
    lane = lax.broadcasted_iota(jnp.int32, (16, 128), 1)

    def send_x(level, f, tiles):
        step = 1 << level
        for i, tile in enumerate(tiles):
            get = lambda k: tile[k * step:k * step + 1, :]
            for way, pair in enumerate(edge_sums(get, 16 // step)):
                for j in range(2):
                    xs[level][way, f, i, j:j + 1, :] = pair[j]

    def both(level, kind, f, act):
        for way in range(2):
            act(exchange(level, kind, f, way))

    start, arrive = lambda copy: copy.start(), lambda copy: copy.wait_recv()

    def spot(i, step):
        return i // step * (8 * step) + i % step

    def packed(step, pairs, pack):
        for i, v in pairs:
            r1, r2 = pltpu.roll(v, step, 1), pltpu.roll(v, 128 - step, 1)
            t = U1 * (v + P1 * (r1 + r2))
            c = jnp.where(lane == 0, v, jnp.where(lane == step, r1 + t, jnp.where(
                lane == 128 - 3 * step, r2 + t, v + P1 * r1)))
            start = i // step * (8 * step)
            here = (lane >= start) & (lane < start + 8 * step) & (lane % step == i % step)
            pack = jnp.where(here, pltpu.roll(c, (spot(i, step) + 3 * step) % 128, 1), pack)
        return pack

    def y_lift(step, i, v, below, above):
        at = spot(i, step)
        def turn(u, k):
            k = (k + 256) % 128
            return u if isinstance(k, int) and k == 0 else pltpu.roll(u, k, 1)
        a, b = turn(below, -at - 2 * step), turn(below, -at)
        c, e = turn(above, -at - 4 * step), turn(above, -at - 5 * step)
        coefs = coefficients(1, step, row, lane)
        return lift_in_place(v, 1, step, a, b, c, e, coefs, lane == 0, lane == 128 - step)

    def planes(f, step, ref):
        return [ref[f * bz + z] if ref is work else ref[f, z] for z in range(0, bz, step)]

    def put(f, step, tiles):
        for i, tile in enumerate(tiles):
            work[f * bz + i * step] = tile

    def loop(body):
        def run(f, carry):
            body(f)
            return carry
        lax.fori_loop(0, n_f, run, 0)

    def stage(level, body, receives, sends):
        def run(fs, f):
            for kind in receives:
                both(level, kind, f, arrive)
            for g in fs:
                body(g)
            for kind in sends:
                both(level, kind, f, start)
        if level == 0:
            loop(lambda f: run([f], f))
        else:
            run(range(n_f), 0)

    def route(part, k):
        w = lax.rem(me + k, groups)
        return pltpu.make_async_remote_copy(
            src_ref=outbox.at[part, w], dst_ref=inbox.at[part, pl.ds(me * (8 * capacity), 8 * capacity)],
            send_sem=a_send.at[part, k], recv_sem=a_recv.at[part, k],
            device_id={"gx": w // n_gy, "gy": lax.rem(w, n_gy)}, device_id_type=MESH)

    def own(part):
        return pltpu.make_async_copy(
            outbox.at[part, me], inbox.at[part, pl.ds(me * (8 * capacity), 8 * capacity)], own_sem.at[part])

    def fill(part, w):
        for r in range(capacity):
            outbox[part, w, 8 * r:8 * r + 8] = work[source_ref[w * capacity + r], pl.ds(part, 8, 2), :]

    def ship(part, first, last):
        def run(k, carry):
            fill(part, lax.rem(me + k, groups))
            route(part, k).start()
            return carry
        lax.fori_loop(first, last, run, 0)

    cuts = [1 + (groups - 1) * i // 4 for i in range(5)]
    work[n_f * bz] = jnp.zeros((16, 128), jnp.float32)
    stage(0, lambda f: send_x(0, f, planes(f, 1, fields_ref)), [], [0])
    for level in range(LEVELS):
        step = 1 << level
        if level > 0:
            ship(1, cuts[2 * level - 2], cuts[2 * level - 1])
        for zway in range(2):
            cs[level][zway] = jnp.zeros((16, 128), jnp.float32)

        def x_stage(f, level=level, step=step):
            coefs = coefficients(0, step, row, lane)
            tiles = planes(f, step, fields_ref if level == 0 else work)
            done = []
            for i, v in enumerate(tiles):
                a, b = [xr[level][0, f, i, j:j + 1, :] for j in range(2)]
                c, e = [xr[level][1, f, i, j:j + 1, :] for j in range(2)]
                done.append(lift_in_place(v, 0, step, a, b, c, e, coefs, row == 0, row == 16 - step))
            put(f, step, done)
            sums = edge_sums(lambda k: done[k], len(done))
            for way in range(2):
                for j in range(2):
                    zs[level][way, f, j] = sums[way][j]
            ys[level][f] = packed(step, list(enumerate(done)), jnp.zeros((16, 128), jnp.float32))
            for way in range(2):
                cs[level][way] = packed(step, [(2 * f + j, sums[way][j]) for j in range(2)], cs[level][way])

        stage(level, x_stage, [0], [2, 1])
        for yway in range(2):
            for zway in range(2):
                corner(level, yway, zway).start()
        if level > 0:
            ship(1, cuts[2 * level - 1], cuts[2 * level])

        def y_stage(f, level=level, step=step):
            below, above = yr[level][0, f], yr[level][1, f]
            put(f, step, [y_lift(step, i, v, below, above) for i, v in enumerate(planes(f, step, work))])

        stage(level, y_stage, [1], [])
        for yway in range(2):
            for zway in range(2):
                corner(level, yway, zway).wait_recv()

        def z_stage(f, level=level, step=step):
            old = planes(f, step, work)
            edge = [[y_lift(step, 2 * f + j, zr[level][way, f, j], cr[level][0, way], cr[level][1, way])
                     for j in range(2)] for way in range(2)]
            new = lift_layers(old, *edge[0], *edge[1])
            if step > 1:
                live = (row % step == 0) & (lane % step == 0)
                new = [jnp.where(live, n, o) for n, o in zip(new, old)]
            put(f, step, new)
            if level + 1 < LEVELS:
                send_x(level + 1, f, new[::2])

        stage(level, z_stage, [2], [])
        if level + 1 < LEVELS:
            both(level + 1, 0, 0, start)

    def gather(k):
        return pltpu.make_async_remote_copy(
            src_ref=gs, dst_ref=gr.at[iz], send_sem=g_send.at[k], recv_sem=g_recv.at[k],
            device_id={"gz": lax.rem(iz + k, n_gz)}, device_id_type=MESH)

    for i in range(2):
        for f in range(n_f):
            for j in range(2):
                low_rows[16 * i + 2 * f + j:16 * i + 2 * f + j + 1, :] = work[f * bz + 8 * i, 8 * j:8 * j + 1, :]
        low_rows[16 * i + 2 * n_f:16 * i + 16, :] = jnp.zeros((16 - 2 * n_f, 128), jnp.float32)
    pick = jnp.where(lax.broadcasted_iota(jnp.int32, (128, 128), 0) ==
                     8 * lax.broadcasted_iota(jnp.int32, (128, 128), 1), jnp.float32(1.0), jnp.float32(0.0))
    gs[...] = jnp.dot(low_rows[...], pick, precision=lax.Precision.HIGHEST, preferred_element_type=jnp.float32)
    for k in range(1, n_gz):
        gather(k).start()
    gr[iz] = gs[...]

    ship(0, 1, groups)
    for part in range(2):
        fill(part, me)
        own(part).start()

    for k in range(1, n_gz):
        gather(k).wait_recv()
    four = lift_whole([gr[g, 16 * i:16 * i + 16, :] for g in range(n_gz) for i in range(2)])
    four[::2] = lift_whole(four[::2])
    for z, tile in enumerate(four):
        for f in range(n_f):
            coarse_ref[f, z] = tile[2 * f:2 * f + 2, :16]

    def finish(k, carry):
        for part in range(2):
            route(part, k).wait()
        return carry

    lax.fori_loop(1, groups, finish, 0)
    for part in range(2):
        own(part).wait()

    def unpack(k, carry):
        for part in range(2):
            for x in range(8):
                at = (2 * x + part) * 128
                received_ref[pl.ds(pl.multiple_of(8 * k, 8), 8), at:at + 128] = (
                    inbox[part, pl.ds(64 * k + x, 8, 8), :])
        return carry

    lax.fori_loop(0, groups * capacity // 8, unpack, 0)
    for k in range(1, n_gz):
        gather(k).wait_send()

    def sent(level, f):
        for kind in range(3):
            both(level, kind, f, lambda copy: copy.wait_send())

    loop(lambda f: sent(0, f))
    for level in range(1, LEVELS):
        sent(level, 0)
    for level in range(LEVELS):
        for yway in range(2):
            for zway in range(2):
                corner(level, yway, zway).wait_send()


def source_table(writers, groups, capacity):
    count = writers.shape[0]
    place = jnp.arange(count, dtype=jnp.int32)
    same = (writers[:, None] == writers[None, :]) & (place[None, :] < place[:, None])
    targets = writers * capacity + jnp.sum(same.astype(jnp.int32), axis=1)
    slots = jnp.arange(groups * capacity, dtype=jnp.int32)
    hit = (targets[None, :] == slots[:, None]).astype(jnp.int32)
    return count - jnp.sum(hit * (count - place)[None, :], axis=1)


def body(fields, tile_writer):
    n_gx, n_gy, n_gz = lax.axis_size("gx"), lax.axis_size("gy"), lax.axis_size("gz")
    n_f, bz, bx, by = fields.shape
    count = n_f * bz
    groups = n_gx * n_gy
    capacity = max(2, 7 * count // (5 * groups) + 1)
    source = source_table(tile_writer.reshape(count), groups, capacity)
    f32 = jnp.float32
    steps = [1 << level for level in range(LEVELS)]
    scratch = [pltpu.VMEM((count + 1, bx, by), f32), pltpu.VMEM((2, groups, 8 * capacity, by), f32),
               pltpu.VMEM((2, groups * 8 * capacity, by), f32)]
    scratch += [pltpu.VMEM((2, n_f, bz // s, 2, by), f32) for s in steps] * 2
    scratch += [pltpu.VMEM((n_f, bx, by), f32) for s in steps]
    scratch += [pltpu.VMEM((2, n_f, bx, by), f32) for s in steps]
    scratch += [pltpu.VMEM((2, n_f, 2, bx, by), f32) for s in steps] * 2
    scratch += [pltpu.VMEM((2, bx, by), f32) for s in steps] + [pltpu.VMEM((2, 2, bx, by), f32) for s in steps]
    scratch += [pltpu.VMEM((32, by), f32)] * 2 + [pltpu.VMEM((n_gz, 32, by), f32)]
    scratch += [pltpu.SemaphoreType.DMA((3 * LEVELS, 2, n_f))] * 2
    scratch += [pltpu.SemaphoreType.DMA((LEVELS, 2, 2))] * 2
    scratch += [pltpu.SemaphoreType.DMA((n_gz,))] * 2 + [pltpu.SemaphoreType.DMA((2, groups))] * 2
    scratch += [pltpu.SemaphoreType.DMA((2,))]
    return pl.pallas_call(
        functools.partial(kernel, (n_gx, n_gy, n_gz, n_f, bz, capacity)),
        out_shape=(jax.ShapeDtypeStruct((n_f, 2 * n_gz, 2, by // 8), f32),
                   jax.ShapeDtypeStruct((groups * capacity, bx * by), f32)),
        in_specs=[pl.BlockSpec(memory_space=pltpu.SMEM), pl.BlockSpec(memory_space=pltpu.VMEM)],
        out_specs=(pl.BlockSpec(memory_space=pltpu.VMEM), pl.BlockSpec(memory_space=pltpu.VMEM)),
        scratch_shapes=scratch,
        compiler_params=pltpu.CompilerParams(collective_id=0, has_side_effects=True,
                                             vmem_limit_bytes=32 * 1024 * 1024),
    )(source, fields)


def solution(mesh):
    return jax.shard_map(
        body,
        mesh=mesh,
        in_specs=(P(None, "gz", "gx", "gy"), P("gx", "gy", "gz", None)),
        out_specs=(P(None, None, "gx", "gy"), P(("gx", "gy"), "gz")),
        check_vma=False,
    )
```

```python
import functools

import jax
import jax.numpy as jnp
import numpy as np
from jax import lax
from jax.experimental import pallas as pl
from jax.experimental.pallas import tpu as pltpu
from jax.sharding import PartitionSpec as P

P1 = -1.586134342059924
U1 = -0.052980118572961
P2 = 0.882911075530934
U2 = 0.443506852043971
LOW = 1.0 / 1.149604398860241
HIGH = 1.149604398860241
LEVELS = 3


def lift_matrix(n, step):
    basis = np.eye(n + 4)
    v, (a, b, c, e) = basis[:n].copy(), basis[n:]
    v[::step] = np.stack(lift_layers(list(v[::step]), a, b, c, e))
    return v


def edge_matrix(n, step):
    below, above = edge_sums(lambda k: np.eye(n)[k * step], n // step)
    return np.stack(below + above)


def tiles_at_once(level):
    return min(8, 16 >> level)


def matrices(level):
    step, t = 1 << level, tiles_at_once(level)
    x_all, x_edge, y_all, y_edge = lift_matrix(16, step), edge_matrix(16, step), lift_matrix(128, step), edge_matrix(128, step)
    mx, hx, ex = np.zeros((128, 128)), np.zeros((128, 32)), np.zeros((32, 128))
    for i in range(t):
        rows = slice(16 * i, 16 * i + 16)
        mx[rows, rows] = x_all[:, :16]
        for way in range(2):
            edge = slice(2 * t * way + 2 * i, 2 * t * way + 2 * i + 2)
            hx[rows, edge] = x_all[:, 16 + 2 * way:18 + 2 * way]
            ex[edge, rows] = x_edge[2 * way:2 * way + 2]
    mq, hy = np.zeros((128, 256)), np.zeros((128, 128))
    mq[:, :128] = y_all[:, :128].T
    for sum_index, offset in enumerate((2, 0, 3, 4)):
        hy[offset * step] = y_all[:, 128 + sum_index]
        for group in range(16):
            mq[:, 128 + group // step * (8 * step) + group % step + offset * step] = y_edge[sum_index]
    return mx, hx, ex, mq, hy


def constant_tables():
    tables = []
    for kind in zip(*[matrices(level) for level in range(LEVELS)]):
        whole = np.stack(kind).astype(np.float32)
        high = whole.astype(jnp.bfloat16)
        low = (whole - high.astype(np.float32)).astype(jnp.bfloat16)
        tables.append(jnp.asarray(np.stack([high, low], axis=1)))
    return tables


def halves(v):
    high = v.astype(jnp.bfloat16)
    return high, (v - high.astype(jnp.float32)).astype(jnp.bfloat16)


def product(a, b):
    dot = lambda p, q: jnp.dot(p, q, preferred_element_type=jnp.float32)
    return dot(a[0], b[0]) + dot(a[1], b[0]) + dot(a[0], b[1])


def edge_sums(get, n):
    a = get(n - 1) + P1 * get(n - 2)
    before = get(n - 3) + P1 * (get(n - 4) + get(n - 2))
    b = get(n - 2) + U1 * before
    c = get(0)
    after = get(1) + P1 * (c + get(2))
    e = c + U1 * after
    return (a, b), (c, e)


def lift_layers(v, a, b, c, e):
    s, d = list(v[0::2]), list(v[1::2])
    n = len(s)
    s_end = [c]
    d = [d[i] + P1 * (s[i] + (s + s_end)[i + 1]) for i in range(n)]
    dm = a + P1 * s[0]
    sm = b + U1 * dm
    s_top = e + U1 * d[-1]
    s = [s[i] + U1 * (([dm] + d)[i] + d[i]) for i in range(n)]
    d = [d[i] + P2 * (s[i] + (s + [s_top])[i + 1]) for i in range(n)]
    dm = dm + P2 * (sm + s[0])
    s = [s[i] + U2 * (([dm] + d)[i] + d[i]) for i in range(n)]
    out = []
    for i in range(n):
        out += [s[i] * LOW, d[i] * HIGH]
    return out


def lift_whole(v):
    s, d = list(v[0::2]), list(v[1::2])
    n = len(s)
    d = [d[i] + P1 * (s[i] + s[(i + 1) % n]) for i in range(n)]
    s = [s[i] + U1 * (d[i - 1] + d[i]) for i in range(n)]
    d = [d[i] + P2 * (s[i] + s[(i + 1) % n]) for i in range(n)]
    s = [s[i] + U2 * (d[i - 1] + d[i]) for i in range(n)]
    out = []
    for i in range(n):
        out += [s[i] * LOW, d[i] * HIGH]
    return out


def kernel(sizes, source_ref, fields_ref, mx_ref, hx_ref, ex_ref, mq_ref, hy_ref, coarse_ref, received_ref, work, outbox, inbox, *scratch):
    n_gx, n_gy, n_gz, n_f, bz, capacity = sizes
    xs, xr, ys, yr, zs, zr, cs, cr = [scratch[LEVELS * i:LEVELS * (i + 1)] for i in range(8)]
    low_rows, gs, gr, send, recv, c_send, c_recv, g_send, g_recv, a_send, a_recv, own_sem = scratch[8 * LEVELS:]
    groups = n_gx * n_gy
    ix, iy, iz = lax.axis_index("gx"), lax.axis_index("gy"), lax.axis_index("gz")
    me = ix * n_gy + iy
    place = {"gx": (ix, n_gx), "gy": (iy, n_gy), "gz": (iz, n_gz)}
    MESH = pl.DeviceIdType.MESH

    def beside(axis, way):
        index, count = place[axis]
        return lax.rem(index + (1 if way == 0 else count - 1), count)

    barrier = pltpu.get_barrier_semaphore()

    def greet_plane(k, carry):
        w = lax.rem(me + k, groups)
        pl.semaphore_signal(barrier, inc=1, device_id={"gx": w // n_gy, "gy": lax.rem(w, n_gy)},
                            device_id_type=MESH)
        return carry

    lax.fori_loop(1, groups, greet_plane, 0)
    for k in range(1, n_gz):
        pl.semaphore_signal(barrier, inc=1, device_id={"gz": lax.rem(iz + k, n_gz)}, device_id_type=MESH)
    for yway in range(2):
        for zway in range(2):
            pl.semaphore_signal(barrier, inc=1, device_id={"gy": beside("gy", yway), "gz": beside("gz", zway)},
                                device_id_type=MESH)
    pl.semaphore_wait(barrier, groups - 1 + n_gz - 1 + 4)

    def exchange(level, kind, f, way):
        axis = ("gx", "gy", "gz")[kind]
        out, into = ((xs, xr), (ys, yr), (zs, zr))[kind]
        src = out[level].at[f] if kind == 1 else out[level].at[way, f]
        row = level * 3 + kind
        return pltpu.make_async_remote_copy(
            src_ref=src, dst_ref=into[level].at[way, f],
            send_sem=send.at[row, way, f], recv_sem=recv.at[row, way, f],
            device_id={axis: beside(axis, way)}, device_id_type=MESH)

    def corner(level, yway, zway):
        return pltpu.make_async_remote_copy(
            src_ref=cs[level].at[zway], dst_ref=cr[level].at[yway, zway],
            send_sem=c_send.at[level, yway, zway], recv_sem=c_recv.at[level, yway, zway],
            device_id={"gy": beside("gy", yway), "gz": beside("gz", zway)}, device_id_type=MESH)

    row = lax.broadcasted_iota(jnp.int32, (16, 128), 0)
    lane = lax.broadcasted_iota(jnp.int32, (16, 128), 1)

    def send_x(level, f, tiles):
        t = tiles_at_once(level)
        sums = tuple(ex_ref[level, half, :4 * t, :16 * t] for half in range(2))
        for k in range(0, len(tiles), t):
            edge = product(sums, halves(jnp.concatenate(tiles[k:k + t], axis=0)))
            for way in range(2):
                xs[level][way, f, 2 * k:2 * (k + t), :] = edge[2 * t * way:2 * t * (way + 1)]
        for way in range(2):
            exchange(level, 0, f, way).start()

    def spot(i, step):
        return i // step * (8 * step) + i % step

    def packed(step, pairs, pack):
        for i, v in pairs:
            start = i // step * (8 * step)
            here = (lane >= start) & (lane < start + 8 * step) & (lane % step == i % step)
            pack = jnp.where(here, v, pack)
        return pack

    def edge_lanes(step, below, above, spots):
        both = jnp.where(lane % (8 * step) // step < 3, below, above)
        return [pltpu.roll(both, (128 - spot(i, step)) % 128, 1) for i in spots]

    def planes(f, step, ref):
        return [ref[f * bz + z] if ref is work else ref[f, z] for z in range(0, bz, step)]

    def put(f, step, tiles):
        for i, tile in enumerate(tiles):
            work[f * bz + i * step] = tile

    def loop(body):
        def run(f, carry):
            body(f)
            return carry
        lax.fori_loop(0, n_f, run, 0)

    def route(part, k):
        w = lax.rem(me + k, groups)
        return pltpu.make_async_remote_copy(
            src_ref=outbox.at[part, w], dst_ref=inbox.at[part, pl.ds(me * (8 * capacity), 8 * capacity)],
            send_sem=a_send.at[part, k], recv_sem=a_recv.at[part, k],
            device_id={"gx": w // n_gy, "gy": lax.rem(w, n_gy)}, device_id_type=MESH)

    def own(part):
        return pltpu.make_async_copy(
            outbox.at[part, me], inbox.at[part, pl.ds(me * (8 * capacity), 8 * capacity)], own_sem.at[part])

    def fill(part, w):
        for r in range(capacity):
            outbox[part, w, 8 * r:8 * r + 8] = work[source_ref[w * capacity + r], pl.ds(part, 8, 2), :]

    def ship(part, first, last):
        def run(k, carry):
            fill(part, lax.rem(me + k, groups))
            route(part, k).start()
            return carry
        lax.fori_loop(first, last, run, 0)

    cuts = [1 + (groups - 1) * i // 4 for i in range(5)]
    work[n_f * bz] = jnp.zeros((16, 128), jnp.float32)
    loop(lambda f: send_x(0, f, planes(f, 1, fields_ref)))
    for level in range(LEVELS):
        step = 1 << level
        if level > 0:
            ship(1, cuts[2 * level - 2], cuts[2 * level - 1])
        for zway in range(2):
            cs[level][zway] = jnp.zeros((16, 128), jnp.float32)

        t = tiles_at_once(level)
        live = (row % step == 0) & (lane % step == 0)

        def x_stage(f, level=level, step=step, t=t, live=live):
            tiles = planes(f, step, fields_ref if level == 0 else work)
            for way in range(2):
                exchange(level, 0, f, way).wait_recv()
            mx = tuple(mx_ref[level, half, :16 * t, :16 * t] for half in range(2))
            hx = tuple(hx_ref[level, half, :16 * t, :4 * t] for half in range(2))
            mq = tuple(mq_ref[level, half] for half in range(2))
            wide = []
            for k in range(0, len(tiles), t):
                edge = jnp.concatenate([xr[level][way, f, 2 * k:2 * (k + t), :] for way in range(2)], axis=0)
                lifted = product(mx, halves(jnp.concatenate(tiles[k:k + t], axis=0))) + product(hx, halves(edge))
                lifted = product(halves(lifted), mq)
                wide += [lifted[16 * i:16 * i + 16] for i in range(t)]
            own_lanes, sum_lanes = [w[:, :128] for w in wide], [w[:, 128:] for w in wide]
            put(f, step, own_lanes if step == 1 else [jnp.where(live, n, o) for n, o in zip(own_lanes, tiles)])
            sums = edge_sums(lambda k: own_lanes[k], len(wide))
            for way in range(2):
                for j in range(2):
                    zs[level][way, f, j] = sums[way][j]
                exchange(level, 2, f, way).start()
            ys[level][f] = packed(step, list(enumerate(sum_lanes)), jnp.zeros((16, 128), jnp.float32))
            for way in range(2):
                exchange(level, 1, f, way).start()
            sums = edge_sums(lambda k: sum_lanes[k], len(wide))
            for way in range(2):
                cs[level][way] = packed(step, [(2 * f + j, sums[way][j]) for j in range(2)], cs[level][way])

        loop(x_stage)
        for yway in range(2):
            for zway in range(2):
                corner(level, yway, zway).start()
        if level > 0:
            ship(1, cuts[2 * level - 1], cuts[2 * level])

        for yway in range(2):
            for zway in range(2):
                corner(level, yway, zway).wait_recv()

        def z_stage(f, level=level, step=step, live=live):
            old = planes(f, step, work)
            for way in range(2):
                exchange(level, 1, f, way).wait_recv()
                exchange(level, 2, f, way).wait_recv()
            hy = tuple(hy_ref[level, half] for half in range(2))
            edges = edge_lanes(step, yr[level][0, f], yr[level][1, f], range(len(old)))
            for way in range(2):
                edges += edge_lanes(step, cr[level][0, way], cr[level][1, way], [2 * f, 2 * f + 1])
            extra = product(halves(jnp.concatenate(edges, axis=0)), hy)
            if step > 1:
                extra = jnp.where((lax.broadcasted_iota(jnp.int32, extra.shape, 0) % step) == 0, extra, 0.0)
            extra = [extra[16 * i:16 * i + 16] for i in range(len(edges))]
            edge = [zr[level][way, f, j] + extra[len(old) + 2 * way + j] for way in range(2) for j in range(2)]
            old = [o + x for o, x in zip(old, extra)]
            new = lift_layers(old, *edge)
            if step > 1:
                new = [jnp.where(live, n, o) for n, o in zip(new, old)]
            put(f, step, new)
            if level + 1 < LEVELS:
                send_x(level + 1, f, new[::2])

        loop(z_stage)

    def gather(k):
        return pltpu.make_async_remote_copy(
            src_ref=gs, dst_ref=gr.at[iz], send_sem=g_send.at[k], recv_sem=g_recv.at[k],
            device_id={"gz": lax.rem(iz + k, n_gz)}, device_id_type=MESH)

    for i in range(2):
        for f in range(n_f):
            for j in range(2):
                low_rows[16 * i + 2 * f + j:16 * i + 2 * f + j + 1, :] = work[f * bz + 8 * i, 8 * j:8 * j + 1, :]
        low_rows[16 * i + 2 * n_f:16 * i + 16, :] = jnp.zeros((16 - 2 * n_f, 128), jnp.float32)
    pick = jnp.where(lax.broadcasted_iota(jnp.int32, (128, 128), 0) ==
                     8 * lax.broadcasted_iota(jnp.int32, (128, 128), 1), jnp.float32(1.0), jnp.float32(0.0))
    gs[...] = jnp.dot(low_rows[...], pick, precision=lax.Precision.HIGHEST, preferred_element_type=jnp.float32)
    for k in range(1, n_gz):
        gather(k).start()
    gr[iz] = gs[...]

    ship(0, 1, groups)
    for part in range(2):
        fill(part, me)
        own(part).start()

    for k in range(1, n_gz):
        gather(k).wait_recv()
    four = lift_whole([gr[g, 16 * i:16 * i + 16, :] for g in range(n_gz) for i in range(2)])
    four[::2] = lift_whole(four[::2])
    for z, tile in enumerate(four):
        for f in range(n_f):
            coarse_ref[f, z] = tile[2 * f:2 * f + 2, :16]

    def finish(k, carry):
        for part in range(2):
            route(part, k).wait()
        return carry

    lax.fori_loop(1, groups, finish, 0)
    for part in range(2):
        own(part).wait()

    def unpack(k, carry):
        for part in range(2):
            for x in range(8):
                at = (2 * x + part) * 128
                received_ref[pl.ds(pl.multiple_of(8 * k, 8), 8), at:at + 128] = (
                    inbox[part, pl.ds(64 * k + x, 8, 8), :])
        return carry

    lax.fori_loop(0, groups * capacity // 8, unpack, 0)
    for k in range(1, n_gz):
        gather(k).wait_send()

    def sent(f):
        for level in range(LEVELS):
            for kind in range(3):
                for way in range(2):
                    exchange(level, kind, f, way).wait_send()

    loop(sent)
    for level in range(LEVELS):
        for yway in range(2):
            for zway in range(2):
                corner(level, yway, zway).wait_send()


def source_table(writers, groups, capacity):
    count = writers.shape[0]
    place = jnp.arange(count, dtype=jnp.int32)
    same = (writers[:, None] == writers[None, :]) & (place[None, :] < place[:, None])
    targets = writers * capacity + jnp.sum(same.astype(jnp.int32), axis=1)
    slots = jnp.arange(groups * capacity, dtype=jnp.int32)
    hit = (targets[None, :] == slots[:, None]).astype(jnp.int32)
    return count - jnp.sum(hit * (count - place)[None, :], axis=1)


def body(fields, tile_writer):
    n_gx, n_gy, n_gz = lax.axis_size("gx"), lax.axis_size("gy"), lax.axis_size("gz")
    n_f, bz, bx, by = fields.shape
    count = n_f * bz
    groups = n_gx * n_gy
    capacity = max(2, 7 * count // (5 * groups) + 1)
    source = source_table(tile_writer.reshape(count), groups, capacity)
    f32 = jnp.float32
    steps = [1 << level for level in range(LEVELS)]
    scratch = [pltpu.VMEM((count + 1, bx, by), f32), pltpu.VMEM((2, groups, 8 * capacity, by), f32),
               pltpu.VMEM((2, groups * 8 * capacity, by), f32)]
    scratch += [pltpu.VMEM((2, n_f, 2 * bz // s, by), f32) for s in steps] * 2
    scratch += [pltpu.VMEM((n_f, bx, by), f32) for s in steps]
    scratch += [pltpu.VMEM((2, n_f, bx, by), f32) for s in steps]
    scratch += [pltpu.VMEM((2, n_f, 2, bx, by), f32) for s in steps] * 2
    scratch += [pltpu.VMEM((2, bx, by), f32) for s in steps] + [pltpu.VMEM((2, 2, bx, by), f32) for s in steps]
    scratch += [pltpu.VMEM((32, by), f32)] * 2 + [pltpu.VMEM((n_gz, 32, by), f32)]
    scratch += [pltpu.SemaphoreType.DMA((3 * LEVELS, 2, n_f))] * 2
    scratch += [pltpu.SemaphoreType.DMA((LEVELS, 2, 2))] * 2
    scratch += [pltpu.SemaphoreType.DMA((n_gz,))] * 2 + [pltpu.SemaphoreType.DMA((2, groups))] * 2
    scratch += [pltpu.SemaphoreType.DMA((2,))]
    return pl.pallas_call(
        functools.partial(kernel, (n_gx, n_gy, n_gz, n_f, bz, capacity)),
        out_shape=(jax.ShapeDtypeStruct((n_f, 2 * n_gz, 2, by // 8), f32),
                   jax.ShapeDtypeStruct((groups * capacity, bx * by), f32)),
        in_specs=[pl.BlockSpec(memory_space=pltpu.SMEM)] + [pl.BlockSpec(memory_space=pltpu.VMEM)] * 6,
        out_specs=(pl.BlockSpec(memory_space=pltpu.VMEM), pl.BlockSpec(memory_space=pltpu.VMEM)),
        scratch_shapes=scratch,
        compiler_params=pltpu.CompilerParams(collective_id=0, has_side_effects=True,
                                             vmem_limit_bytes=32 * 1024 * 1024),
    )(source, fields, *constant_tables())


def solution(mesh):
    return jax.shard_map(
        body,
        mesh=mesh,
        in_specs=(P(None, "gz", "gx", "gy"), P("gx", "gy", "gz", None)),
        out_specs=(P(None, None, "gx", "gy"), P(("gx", "gy"), "gz")),
        check_vma=False,
    )
```

```python
import functools

import jax
import jax.numpy as jnp
import numpy as np
from jax import lax
from jax.experimental import pallas as pl
from jax.experimental.pallas import tpu as pltpu
from jax.sharding import PartitionSpec as P

P1 = -1.586134342059924
U1 = -0.052980118572961
P2 = 0.882911075530934
U2 = 0.443506852043971
LOW = 1.0 / 1.149604398860241
HIGH = 1.149604398860241
LEVELS = 3
PARTS = ((1, 8, 2), (2, 4, 4), (0, 4, 4))


def lift_matrix(n, step):
    basis = np.eye(n + 4)
    v, (a, b, c, e) = basis[:n].copy(), basis[n:]
    v[::step] = np.stack(lift_layers(list(v[::step]), a, b, c, e))
    return v


def edge_matrix(n, step):
    below, above = edge_sums(lambda k: np.eye(n)[k * step], n // step)
    return np.stack(below + above)


def tiles_at_once(level):
    return min(8, 16 >> level)


def matrices(level):
    step, t = 1 << level, tiles_at_once(level)
    x_all, x_edge, y_all, y_edge = lift_matrix(16, step), edge_matrix(16, step), lift_matrix(128, step), edge_matrix(128, step)
    mx, hx, ex = np.zeros((128, 128)), np.zeros((128, 32)), np.zeros((32, 128))
    for i in range(t):
        rows = slice(16 * i, 16 * i + 16)
        mx[rows, rows] = x_all[:, :16]
        for way in range(2):
            edge = slice(2 * t * way + 2 * i, 2 * t * way + 2 * i + 2)
            hx[rows, edge] = x_all[:, 16 + 2 * way:18 + 2 * way]
            ex[edge, rows] = x_edge[2 * way:2 * way + 2]
    mq, hy = np.zeros((128, 256)), np.zeros((128, 128))
    mq[:, :128] = y_all[:, :128].T
    for sum_index, offset in enumerate((2, 0, 3, 4)):
        hy[offset * step] = y_all[:, 128 + sum_index]
        for group in range(16):
            mq[:, 128 + group // step * (8 * step) + group % step + offset * step] = y_edge[sum_index]
    return mx, hx, ex, mq, hy


def constant_tables():
    tables = []
    for kind in zip(*[matrices(level) for level in range(LEVELS)]):
        whole = np.stack(kind).astype(np.float32)
        high = whole.astype(jnp.bfloat16)
        low = (whole - high.astype(np.float32)).astype(jnp.bfloat16)
        tables.append(jnp.asarray(np.stack([high, low], axis=1)))
    return tables


def halves(v):
    high = v.astype(jnp.bfloat16)
    return high, (v - high.astype(jnp.float32)).astype(jnp.bfloat16)


def product(a, b):
    dot = lambda p, q: jnp.dot(p, q, preferred_element_type=jnp.float32)
    return dot(a[0], b[0]) + dot(a[1], b[0]) + dot(a[0], b[1])


def edge_sums(get, n):
    a = get(n - 1) + P1 * get(n - 2)
    before = get(n - 3) + P1 * (get(n - 4) + get(n - 2))
    b = get(n - 2) + U1 * before
    c = get(0)
    after = get(1) + P1 * (c + get(2))
    e = c + U1 * after
    return (a, b), (c, e)


def lift_layers(v, a, b, c, e):
    s, d = list(v[0::2]), list(v[1::2])
    n = len(s)
    s_end = [c]
    d = [d[i] + P1 * (s[i] + (s + s_end)[i + 1]) for i in range(n)]
    dm = a + P1 * s[0]
    sm = b + U1 * dm
    s_top = e + U1 * d[-1]
    s = [s[i] + U1 * (([dm] + d)[i] + d[i]) for i in range(n)]
    d = [d[i] + P2 * (s[i] + (s + [s_top])[i + 1]) for i in range(n)]
    dm = dm + P2 * (sm + s[0])
    s = [s[i] + U2 * (([dm] + d)[i] + d[i]) for i in range(n)]
    out = []
    for i in range(n):
        out += [s[i] * LOW, d[i] * HIGH]
    return out


def lift_whole(v):
    s, d = list(v[0::2]), list(v[1::2])
    n = len(s)
    d = [d[i] + P1 * (s[i] + s[(i + 1) % n]) for i in range(n)]
    s = [s[i] + U1 * (d[i - 1] + d[i]) for i in range(n)]
    d = [d[i] + P2 * (s[i] + s[(i + 1) % n]) for i in range(n)]
    s = [s[i] + U2 * (d[i - 1] + d[i]) for i in range(n)]
    out = []
    for i in range(n):
        out += [s[i] * LOW, d[i] * HIGH]
    return out


def kernel(sizes, source_ref, *refs):
    n_gx, n_gy, n_gz, n_f, bz, capacity = sizes
    given, (coarse_ref, received_ref), held, scratch = refs[:6], refs[6:8], refs[8:14], refs[14:]
    fields_ref, mx_ref, hx_ref, ex_ref, mq_ref, hy_ref = held
    work, turn_rows, load_sem = scratch[:3]
    outbox, inbox, scratch = scratch[3:6], scratch[6:9], scratch[9:]
    loads = [pltpu.make_async_copy(a, b, load_sem.at[i]) for i, (a, b) in enumerate(zip(given, held))]
    for load in loads:
        load.start()
    xs, xr, ys, yr, zs, zr, cs, cr = [scratch[LEVELS * i:LEVELS * (i + 1)] for i in range(8)]
    low_rows, gs, gr, send, recv, c_send, c_recv, g_send, g_recv, a_send, a_recv, own_sem = scratch[8 * LEVELS:]
    groups = n_gx * n_gy
    ix, iy, iz = lax.axis_index("gx"), lax.axis_index("gy"), lax.axis_index("gz")
    me = ix * n_gy + iy
    place = {"gx": (ix, n_gx), "gy": (iy, n_gy), "gz": (iz, n_gz)}
    MESH = pl.DeviceIdType.MESH

    def beside(axis, way):
        index, count = place[axis]
        return lax.rem(index + (1 if way == 0 else count - 1), count)

    barrier = pltpu.get_barrier_semaphore()

    def greet_plane(k, carry):
        w = lax.rem(me + k, groups)
        pl.semaphore_signal(barrier, inc=1, device_id={"gx": w // n_gy, "gy": lax.rem(w, n_gy)},
                            device_id_type=MESH)
        return carry

    lax.fori_loop(1, groups, greet_plane, 0)
    for k in range(1, n_gz):
        pl.semaphore_signal(barrier, inc=1, device_id={"gz": lax.rem(iz + k, n_gz)}, device_id_type=MESH)
    for yway in range(2):
        for zway in range(2):
            pl.semaphore_signal(barrier, inc=1, device_id={"gy": beside("gy", yway), "gz": beside("gz", zway)},
                                device_id_type=MESH)
    for load in loads:
        load.wait()
    pl.semaphore_wait(barrier, groups - 1 + n_gz - 1 + 4)

    def exchange(level, kind, f, way):
        axis = ("gx", "gy", "gz")[kind]
        out, into = ((xs, xr), (ys, yr), (zs, zr))[kind]
        src = out[level].at[f] if kind == 1 else out[level].at[way, f]
        row = level * 3 + kind
        return pltpu.make_async_remote_copy(
            src_ref=src, dst_ref=into[level].at[way, f],
            send_sem=send.at[row, way, f], recv_sem=recv.at[row, way, f],
            device_id={axis: beside(axis, way)}, device_id_type=MESH)

    def corner(level, yway, zway):
        return pltpu.make_async_remote_copy(
            src_ref=cs[level].at[zway], dst_ref=cr[level].at[yway, zway],
            send_sem=c_send.at[level, yway, zway], recv_sem=c_recv.at[level, yway, zway],
            device_id={"gy": beside("gy", yway), "gz": beside("gz", zway)}, device_id_type=MESH)

    row = lax.broadcasted_iota(jnp.int32, (16, 128), 0)
    lane = lax.broadcasted_iota(jnp.int32, (16, 128), 1)

    def send_x(level, f, tiles):
        t = tiles_at_once(level)
        sums = tuple(ex_ref[level, half, :4 * t, :16 * t] for half in range(2))
        for k in range(0, len(tiles), t):
            edge = product(sums, halves(jnp.concatenate(tiles[k:k + t], axis=0)))
            for way in range(2):
                xs[level][way, f, 2 * k:2 * (k + t), :] = edge[2 * t * way:2 * t * (way + 1)]
        for way in range(2):
            exchange(level, 0, f, way).start()

    def spot(i, step):
        return i // step * (8 * step) + i % step

    def packed(step, pairs, pack):
        for i, v in pairs:
            start = i // step * (8 * step)
            here = (lane >= start) & (lane < start + 8 * step) & (lane % step == i % step)
            pack = jnp.where(here, v, pack)
        return pack

    def edge_lanes(step, below, above, spots):
        both = jnp.where(lane % (8 * step) // step < 3, below, above)
        return [pltpu.roll(both, (128 - spot(i, step)) % 128, 1) for i in spots]

    def planes(f, step, ref):
        return [ref[f * bz + z] if ref is work else ref[f, z] for z in range(0, bz, step)]

    def put(f, step, tiles):
        for i, tile in enumerate(tiles):
            work[f * bz + i * step] = tile

    def loop(body):
        def run(f, carry):
            body(f)
            return carry
        lax.fori_loop(0, n_f, run, 0)

    def squeeze(slot, v, step):
        if step == 1:
            return v
        turn_rows[slot] = v
        return turn_rows[slot, pl.ds(0, 16 // step, step), :]

    def spread(slot, v, step):
        if step == 1:
            return v
        turn_rows[slot, pl.ds(0, 16 // step, step), :] = v
        return turn_rows[slot]

    def route(part, k):
        w = lax.rem(me + k, groups)
        return pltpu.make_async_remote_copy(
            src_ref=outbox[part].at[w], dst_ref=inbox[part].at[pl.ds(me * capacity, capacity)],
            send_sem=a_send.at[part, k], recv_sem=a_recv.at[part, k],
            device_id={"gx": w // n_gy, "gy": lax.rem(w, n_gy)}, device_id_type=MESH)

    def own(part):
        return pltpu.make_async_copy(
            outbox[part].at[me], inbox[part].at[pl.ds(me * capacity, capacity)], own_sem.at[part])

    def fill(part, w):
        first, count, stride = PARTS[part]
        for r in range(capacity):
            outbox[part][w, r] = work[source_ref[w * capacity + r], pl.ds(first, count, stride), :]

    def ship(part, first, last):
        def run(k, carry):
            fill(part, lax.rem(me + k, groups))
            route(part, k).start()
            return carry
        lax.fori_loop(first, last, run, 0)

    cuts = [1 + (groups - 1) * i // 2 for i in range(3)]
    turn_rows[...] = jnp.zeros_like(turn_rows)
    work[n_f * bz] = jnp.zeros((16, 128), jnp.float32)
    loop(lambda f: send_x(0, f, planes(f, 1, fields_ref)))
    for level in range(LEVELS):
        step = 1 << level
        if level > 0:
            ship(level - 1, cuts[0], cuts[1])
        for zway in range(2):
            cs[level][zway] = jnp.zeros((16, 128), jnp.float32)

        t = tiles_at_once(level)
        live = (row % step == 0) & (lane % step == 0)

        def x_stage(f, level=level, step=step, t=t, live=live):
            tiles = planes(f, step, fields_ref if level == 0 else work)
            for way in range(2):
                exchange(level, 0, f, way).wait_recv()
            mx = tuple(mx_ref[level, half, :16 * t, :16 * t] for half in range(2))
            hx = tuple(hx_ref[level, half, :16 * t, :4 * t] for half in range(2))
            mq = tuple(mq_ref[level, half] for half in range(2))
            wide = []
            for k in range(0, len(tiles), t):
                edge = jnp.concatenate([xr[level][way, f, 2 * k:2 * (k + t), :] for way in range(2)], axis=0)
                lifted = product(mx, halves(jnp.concatenate(tiles[k:k + t], axis=0))) + product(hx, halves(edge))
                lifted = product(halves(lifted), mq)
                wide += [lifted[16 * i:16 * i + 16] for i in range(t)]
            own_lanes, sum_lanes = [w[:, :128] for w in wide], [w[:, 128:] for w in wide]
            put(f, step, own_lanes if step == 1 else [jnp.where(live, n, o) for n, o in zip(own_lanes, tiles)])
            sums = edge_sums(lambda k: own_lanes[k], len(wide))
            for way in range(2):
                if step == 1:
                    for j in range(2):
                        zs[level][way, f, j] = sums[way][j]
                else:
                    mixed = jnp.where(lane % step == 0, sums[way][0], pltpu.roll(sums[way][1], 1, 1))
                    zs[level][way, f] = squeeze(way, mixed, step)
                exchange(level, 2, f, way).start()
            pack = packed(step, list(enumerate(sum_lanes)), jnp.zeros((16, 128), jnp.float32))
            ys[level][f] = squeeze(2, pack, step)
            for way in range(2):
                exchange(level, 1, f, way).start()
            sums = edge_sums(lambda k: sum_lanes[k], len(wide))
            for way in range(2):
                cs[level][way] = packed(step, [(2 * f + j, sums[way][j]) for j in range(2)], cs[level][way])

        loop(x_stage)
        for yway in range(2):
            for zway in range(2):
                corner(level, yway, zway).start()
        if level > 0:
            ship(level - 1, cuts[1], cuts[2])
            fill(level - 1, me)
            own(level - 1).start()

        for yway in range(2):
            for zway in range(2):
                corner(level, yway, zway).wait_recv()

        def z_stage(f, level=level, step=step, live=live):
            old = planes(f, step, work)
            for way in range(2):
                exchange(level, 1, f, way).wait_recv()
                exchange(level, 2, f, way).wait_recv()
            hy = tuple(hy_ref[level, half] for half in range(2))
            edges = edge_lanes(step, spread(3, yr[level][0, f], step), spread(4, yr[level][1, f], step), range(len(old)))
            for way in range(2):
                edges += edge_lanes(step, cr[level][0, way], cr[level][1, way], [2 * f, 2 * f + 1])
            extra = product(halves(jnp.concatenate(edges, axis=0)), hy)
            if step > 1:
                extra = jnp.where((lax.broadcasted_iota(jnp.int32, extra.shape, 0) % step) == 0, extra, 0.0)
            extra = [extra[16 * i:16 * i + 16] for i in range(len(edges))]
            far = []
            for way in range(2):
                if step == 1:
                    far += [zr[level][way, f, 0], zr[level][way, f, 1]]
                else:
                    mixed = spread(5 + way, zr[level][way, f], step)
                    far += [mixed, pltpu.roll(mixed, 127, 1)]
            edge = [v + x for v, x in zip(far, extra[len(old):])]
            old = [o + x for o, x in zip(old, extra)]
            new = lift_layers(old, *edge)
            if step > 1:
                new = [jnp.where(live, n, o) for n, o in zip(new, old)]
            put(f, step, new)
            if level + 1 < LEVELS:
                send_x(level + 1, f, new[::2])

        loop(z_stage)

    def gather(k):
        return pltpu.make_async_remote_copy(
            src_ref=gs, dst_ref=gr.at[iz], send_sem=g_send.at[k], recv_sem=g_recv.at[k],
            device_id={"gz": lax.rem(iz + k, n_gz)}, device_id_type=MESH)

    for i in range(2):
        for f in range(n_f):
            for j in range(2):
                low_rows[16 * i + 2 * f + j:16 * i + 2 * f + j + 1, :] = work[f * bz + 8 * i, 8 * j:8 * j + 1, :]
        low_rows[16 * i + 2 * n_f:16 * i + 16, :] = jnp.zeros((16 - 2 * n_f, 128), jnp.float32)
    pick = jnp.where(lax.broadcasted_iota(jnp.int32, (128, 128), 0) ==
                     8 * lax.broadcasted_iota(jnp.int32, (128, 128), 1), jnp.float32(1.0), jnp.float32(0.0))
    gs[...] = jnp.dot(low_rows[...], pick, precision=lax.Precision.HIGHEST, preferred_element_type=jnp.float32)
    for k in range(1, n_gz):
        gather(k).start()
    gr[iz] = gs[...]

    last = len(PARTS) - 1
    ship(last, 1, groups)
    fill(last, me)
    own(last).start()

    for k in range(1, n_gz):
        gather(k).wait_recv()
    four = lift_whole([gr[g, 16 * i:16 * i + 16, :] for g in range(n_gz) for i in range(2)])
    four[::2] = lift_whole(four[::2])
    for z, tile in enumerate(four):
        for f in range(n_f):
            coarse_ref[f, z] = tile[2 * f:2 * f + 2, :16]

    def finish(k, carry):
        for part in range(len(PARTS)):
            route(part, k).wait()
        return carry

    lax.fori_loop(1, groups, finish, 0)
    for part in range(len(PARTS)):
        own(part).wait()

    def unpack(k, carry):
        for part, (first, count, stride) in enumerate(PARTS):
            for x in range(count):
                at = (first + stride * x) * 128
                received_ref[pl.ds(pl.multiple_of(8 * k, 8), 8), at:at + 128] = inbox[part][pl.ds(8 * k, 8), x, :]
        return carry

    lax.fori_loop(0, groups * capacity // 8, unpack, 0)
    for k in range(1, n_gz):
        gather(k).wait_send()

    def sent(f):
        for level in range(LEVELS):
            for kind in range(3):
                for way in range(2):
                    exchange(level, kind, f, way).wait_send()

    loop(sent)
    for level in range(LEVELS):
        for yway in range(2):
            for zway in range(2):
                corner(level, yway, zway).wait_send()


def source_table(writers, groups, capacity):
    count = writers.shape[0]
    place = jnp.arange(count, dtype=jnp.int32)
    same = (writers[:, None] == writers[None, :]) & (place[None, :] < place[:, None])
    targets = writers * capacity + jnp.sum(same.astype(jnp.int32), axis=1)
    slots = jnp.arange(groups * capacity, dtype=jnp.int32)
    hit = (targets[None, :] == slots[:, None]).astype(jnp.int32)
    return count - jnp.sum(hit * (count - place)[None, :], axis=1)


def body(fields, tile_writer):
    n_gx, n_gy, n_gz = lax.axis_size("gx"), lax.axis_size("gy"), lax.axis_size("gz")
    n_f, bz, bx, by = fields.shape
    count = n_f * bz
    groups = n_gx * n_gy
    capacity = max(2, 7 * count // (5 * groups) + 1)
    source = source_table(tile_writer.reshape(count), groups, capacity)
    f32 = jnp.float32
    steps = [1 << level for level in range(LEVELS)]
    tables = constant_tables()
    scratch = [pltpu.VMEM(a.shape, a.dtype) for a in (fields, *tables)]
    scratch += [pltpu.VMEM((count + 1, bx, by), f32), pltpu.VMEM((7, bx, by), f32), pltpu.SemaphoreType.DMA((6,))]
    scratch += [pltpu.VMEM((groups, capacity, p[1], by), f32) for p in PARTS]
    scratch += [pltpu.VMEM((groups * capacity, p[1], by), f32) for p in PARTS]
    scratch += [pltpu.VMEM((2, n_f, 2 * bz // s, by), f32) for s in steps] * 2
    scratch += [pltpu.VMEM((n_f, bx // s, by), f32) for s in steps]
    scratch += [pltpu.VMEM((2, n_f, bx // s, by), f32) for s in steps]
    scratch += [pltpu.VMEM((2, n_f, 2, bx, by) if s == 1 else (2, n_f, bx // s, by), f32) for s in steps] * 2
    scratch += [pltpu.VMEM((2, bx, by), f32) for s in steps] + [pltpu.VMEM((2, 2, bx, by), f32) for s in steps]
    scratch += [pltpu.VMEM((32, by), f32)] * 2 + [pltpu.VMEM((n_gz, 32, by), f32)]
    scratch += [pltpu.SemaphoreType.DMA((3 * LEVELS, 2, n_f))] * 2
    scratch += [pltpu.SemaphoreType.DMA((LEVELS, 2, 2))] * 2
    scratch += [pltpu.SemaphoreType.DMA((n_gz,))] * 2 + [pltpu.SemaphoreType.DMA((len(PARTS), groups))] * 2
    scratch += [pltpu.SemaphoreType.DMA((len(PARTS),))]
    return pl.pallas_call(
        functools.partial(kernel, (n_gx, n_gy, n_gz, n_f, bz, capacity)),
        out_shape=(jax.ShapeDtypeStruct((n_f, 2 * n_gz, 2, by // 8), f32),
                   jax.ShapeDtypeStruct((groups * capacity, bx * by), f32)),
        in_specs=[pl.BlockSpec(memory_space=pltpu.SMEM)] + [pl.BlockSpec(memory_space=pl.ANY)] * 6,
        out_specs=(pl.BlockSpec(memory_space=pltpu.VMEM), pl.BlockSpec(memory_space=pltpu.VMEM)),
        scratch_shapes=scratch,
        compiler_params=pltpu.CompilerParams(collective_id=0, has_side_effects=True,
                                             vmem_limit_bytes=32 * 1024 * 1024),
    )(source, fields, *tables)


def solution(mesh):
    return jax.shard_map(
        body,
        mesh=mesh,
        in_specs=(P(None, "gz", "gx", "gy"), P("gx", "gy", "gz", None)),
        out_specs=(P(None, None, "gx", "gy"), P(("gx", "gy"), "gz")),
        check_vma=False,
    )
```

```python
import functools

import jax
import jax.numpy as jnp
import numpy as np
from jax import lax
from jax.experimental import pallas as pl
from jax.experimental.pallas import tpu as pltpu
from jax.sharding import PartitionSpec as P

P1 = -1.586134342059924
U1 = -0.052980118572961
P2 = 0.882911075530934
U2 = 0.443506852043971
LOW = 1.0 / 1.149604398860241
HIGH = 1.149604398860241
LEVELS = 3
PARTS = ((1, 8, 2), (2, 4, 4), (0, 4, 4))


def lift_matrix(n, step):
    basis = np.eye(n + 4)
    v, (a, b, c, e) = basis[:n].copy(), basis[n:]
    v[::step] = np.stack(lift_layers(list(v[::step]), a, b, c, e))
    return v


def edge_matrix(n, step):
    below, above = edge_sums(lambda k: np.eye(n)[k * step], n // step)
    return np.stack(below + above)


def tiles_at_once(level):
    return min(8, 16 >> level)


def matrices(level):
    step, t = 1 << level, tiles_at_once(level)
    x_all, x_edge, y_all, y_edge = lift_matrix(16, step), edge_matrix(16, step), lift_matrix(128, step), edge_matrix(128, step)
    mx, hx, ex = np.zeros((128, 128)), np.zeros((128, 32)), np.zeros((32, 128))
    for i in range(t):
        rows = slice(16 * i, 16 * i + 16)
        mx[rows, rows] = x_all[:, :16]
        for way in range(2):
            edge = slice(2 * t * way + 2 * i, 2 * t * way + 2 * i + 2)
            hx[rows, edge] = x_all[:, 16 + 2 * way:18 + 2 * way]
            ex[edge, rows] = x_edge[2 * way:2 * way + 2]
    mq, hy = np.zeros((128, 256)), np.zeros((128, 128))
    mq[:, :128] = y_all[:, :128].T
    for sum_index, offset in enumerate((2, 0, 3, 4)):
        hy[offset * step] = y_all[:, 128 + sum_index]
        for group in range(16):
            mq[:, 128 + group // step * (8 * step) + group % step + offset * step] = y_edge[sum_index]
    return mx, hx, ex, mq, hy


def constant_tables():
    tables = []
    for kind in zip(*[matrices(level) for level in range(LEVELS)]):
        whole = np.stack(kind).astype(np.float32)
        high = whole.astype(jnp.bfloat16)
        low = (whole - high.astype(np.float32)).astype(jnp.bfloat16)
        tables.append(jnp.asarray(np.stack([high, low], axis=1)))
    return tables


def halves(v):
    high = v.astype(jnp.bfloat16)
    return high, (v - high.astype(jnp.float32)).astype(jnp.bfloat16)


def product(a, b):
    dot = lambda p, q: jnp.dot(p, q, preferred_element_type=jnp.float32)
    return dot(a[0], b[0]) + dot(a[1], b[0]) + dot(a[0], b[1])


def edge_sums(get, n):
    a = get(n - 1) + P1 * get(n - 2)
    before = get(n - 3) + P1 * (get(n - 4) + get(n - 2))
    b = get(n - 2) + U1 * before
    c = get(0)
    after = get(1) + P1 * (c + get(2))
    e = c + U1 * after
    return (a, b), (c, e)


def lift_layers(v, a, b, c, e):
    s, d = list(v[0::2]), list(v[1::2])
    n = len(s)
    s_end = [c]
    d = [d[i] + P1 * (s[i] + (s + s_end)[i + 1]) for i in range(n)]
    dm = a + P1 * s[0]
    sm = b + U1 * dm
    s_top = e + U1 * d[-1]
    s = [s[i] + U1 * (([dm] + d)[i] + d[i]) for i in range(n)]
    d = [d[i] + P2 * (s[i] + (s + [s_top])[i + 1]) for i in range(n)]
    dm = dm + P2 * (sm + s[0])
    s = [s[i] + U2 * (([dm] + d)[i] + d[i]) for i in range(n)]
    out = []
    for i in range(n):
        out += [s[i] * LOW, d[i] * HIGH]
    return out


def lift_whole(v):
    s, d = list(v[0::2]), list(v[1::2])
    n = len(s)
    d = [d[i] + P1 * (s[i] + s[(i + 1) % n]) for i in range(n)]
    s = [s[i] + U1 * (d[i - 1] + d[i]) for i in range(n)]
    d = [d[i] + P2 * (s[i] + s[(i + 1) % n]) for i in range(n)]
    s = [s[i] + U2 * (d[i - 1] + d[i]) for i in range(n)]
    out = []
    for i in range(n):
        out += [s[i] * LOW, d[i] * HIGH]
    return out


def kernel(sizes, source_ref, *refs):
    n_gx, n_gy, n_gz, n_f, bz, capacity = sizes
    given, (coarse_ref, received_ref), held, scratch = refs[:6], refs[6:8], refs[8:14], refs[14:]
    fields_ref, mx_ref, hx_ref, ex_ref, mq_ref, hy_ref = held
    work, turn_rows, load_sem = scratch[:3]
    outbox, inbox, scratch = scratch[3:6], scratch[6:9], scratch[9:]
    loads = [pltpu.make_async_copy(a, b, load_sem.at[i]) for i, (a, b) in enumerate(zip(given, held))]
    for load in loads:
        load.start()
    xs, xr, ys, yr, zs, zr, cs, cr = [scratch[LEVELS * i:LEVELS * (i + 1)] for i in range(8)]
    low_rows, gs, gr, send, recv, c_send, c_recv, g_send, g_recv, a_send, a_recv, own_sem = scratch[8 * LEVELS:]
    groups = n_gx * n_gy
    ix, iy, iz = lax.axis_index("gx"), lax.axis_index("gy"), lax.axis_index("gz")
    me = ix * n_gy + iy
    place = {"gx": (ix, n_gx), "gy": (iy, n_gy), "gz": (iz, n_gz)}
    MESH = pl.DeviceIdType.MESH

    def beside(axis, way):
        index, count = place[axis]
        return lax.rem(index + (1 if way == 0 else count - 1), count)

    barrier = pltpu.get_barrier_semaphore()

    def greet_plane(k, carry):
        w = lax.rem(me + k, groups)
        pl.semaphore_signal(barrier, inc=1, device_id={"gx": w // n_gy, "gy": lax.rem(w, n_gy)},
                            device_id_type=MESH)
        return carry

    lax.fori_loop(1, groups, greet_plane, 0)
    for k in range(1, n_gz):
        pl.semaphore_signal(barrier, inc=1, device_id={"gz": lax.rem(iz + k, n_gz)}, device_id_type=MESH)
    for yway in range(2):
        for zway in range(2):
            pl.semaphore_signal(barrier, inc=1, device_id={"gy": beside("gy", yway), "gz": beside("gz", zway)},
                                device_id_type=MESH)
    for load in loads:
        load.wait()
    pl.semaphore_wait(barrier, groups - 1 + n_gz - 1 + 4)

    def exchange(level, kind, f, way):
        axis = ("gx", "gy", "gz")[kind]
        out, into = ((xs, xr), (ys, yr), (zs, zr))[kind]
        src = out[level].at[f] if kind == 1 else out[level].at[way, f]
        row = level * 3 + kind
        return pltpu.make_async_remote_copy(
            src_ref=src, dst_ref=into[level].at[way, f],
            send_sem=send.at[row, way, f], recv_sem=recv.at[row, way, f],
            device_id={axis: beside(axis, way)}, device_id_type=MESH)

    def corner(level, yway, zway):
        return pltpu.make_async_remote_copy(
            src_ref=cs[level].at[zway], dst_ref=cr[level].at[yway, zway],
            send_sem=c_send.at[level, yway, zway], recv_sem=c_recv.at[level, yway, zway],
            device_id={"gy": beside("gy", yway), "gz": beside("gz", zway)}, device_id_type=MESH)

    row = lax.broadcasted_iota(jnp.int32, (16, 128), 0)
    lane = lax.broadcasted_iota(jnp.int32, (16, 128), 1)

    def send_x(level, f, tiles):
        t = tiles_at_once(level)
        sums = tuple(ex_ref[level, half, :4 * t, :16 * t] for half in range(2))
        for k in range(0, len(tiles), t):
            edge = product(sums, halves(jnp.concatenate(tiles[k:k + t], axis=0)))
            for way in range(2):
                xs[level][way, f, 2 * k:2 * (k + t), :] = edge[2 * t * way:2 * t * (way + 1)]
        for way in range(2):
            exchange(level, 0, f, way).start()

    def spot(i, step):
        return i // step * (8 * step) + i % step

    def packed(step, pairs, pack):
        for i, v in pairs:
            start = i // step * (8 * step)
            here = (lane >= start) & (lane < start + 8 * step) & (lane % step == i % step)
            pack = jnp.where(here, v, pack)
        return pack

    def edge_lanes(step, below, above, spots):
        both = jnp.where(lane % (8 * step) // step < 3, below, above)
        return [pltpu.roll(both, (128 - spot(i, step)) % 128, 1) for i in spots]

    def planes(f, step, ref):
        return [ref[f * bz + z] if ref is work else ref[f, z] for z in range(0, bz, step)]

    def put(f, step, tiles):
        for i, tile in enumerate(tiles):
            work[f * bz + i * step] = tile

    def loop(body):
        def run(f, carry):
            body(f)
            return carry
        lax.fori_loop(0, n_f, run, 0)

    def squeeze(slot, v, step):
        if step == 1:
            return v
        turn_rows[slot] = v
        return turn_rows[slot, pl.ds(0, 16 // step, step), :]

    def spread(slot, v, step):
        if step == 1:
            return v
        turn_rows[slot, pl.ds(0, 16 // step, step), :] = v
        return turn_rows[slot]

    def route(part, k):
        w = lax.rem(me + k, groups)
        return pltpu.make_async_remote_copy(
            src_ref=outbox[part].at[w], dst_ref=inbox[part].at[pl.ds(me * capacity, capacity)],
            send_sem=a_send.at[part, k], recv_sem=a_recv.at[part, k],
            device_id={"gx": w // n_gy, "gy": lax.rem(w, n_gy)}, device_id_type=MESH)

    def own(part):
        return pltpu.make_async_copy(
            outbox[part].at[me], inbox[part].at[pl.ds(me * capacity, capacity)], own_sem.at[part])

    def fill(part, w):
        first, count, stride = PARTS[part]
        for r in range(capacity):
            outbox[part][w, r] = work[source_ref[w * capacity + r], pl.ds(first, count, stride), :]

    def ship(part, first, last):
        def run(k, carry):
            fill(part, lax.rem(me + k, groups))
            route(part, k).start()
            return carry
        lax.fori_loop(first, last, run, 0)

    cuts = [1 + (groups - 1) * i // 2 for i in range(3)]
    turn_rows[...] = jnp.zeros_like(turn_rows)
    work[n_f * bz] = jnp.zeros((16, 128), jnp.float32)
    loop(lambda f: send_x(0, f, planes(f, 1, fields_ref)))
    for level in range(LEVELS):
        step = 1 << level
        if level > 0:
            ship(level - 1, cuts[0], cuts[1])
        for zway in range(2):
            cs[level][zway] = jnp.zeros((16, 128), jnp.float32)

        t = tiles_at_once(level)
        live = (row % step == 0) & (lane % step == 0)

        def x_stage(f, level=level, step=step, t=t, live=live):
            tiles = planes(f, step, fields_ref if level == 0 else work)
            for way in range(2):
                exchange(level, 0, f, way).wait_recv()
            mx = tuple(mx_ref[level, half, :16 * t, :16 * t] for half in range(2))
            hx = tuple(hx_ref[level, half, :16 * t, :4 * t] for half in range(2))
            mq = tuple(mq_ref[level, half] for half in range(2))
            wide = []
            for k in range(0, len(tiles), t):
                edge = jnp.concatenate([xr[level][way, f, 2 * k:2 * (k + t), :] for way in range(2)], axis=0)
                lifted = product(mx, halves(jnp.concatenate(tiles[k:k + t], axis=0))) + product(hx, halves(edge))
                lifted = product(halves(lifted), mq)
                wide += [lifted[16 * i:16 * i + 16] for i in range(t)]
            own_lanes, sum_lanes = [w[:, :128] for w in wide], [w[:, 128:] for w in wide]
            put(f, step, own_lanes if step == 1 else [jnp.where(live, n, o) for n, o in zip(own_lanes, tiles)])
            sums = edge_sums(lambda k: own_lanes[k], len(wide))
            for way in range(2):
                if step == 1:
                    for j in range(2):
                        zs[level][way, f, j] = sums[way][j]
                else:
                    mixed = jnp.where(lane % step == 0, sums[way][0], pltpu.roll(sums[way][1], 1, 1))
                    zs[level][way, f] = squeeze(way, mixed, step)
                exchange(level, 2, f, way).start()
            pack = packed(step, list(enumerate(sum_lanes)), jnp.zeros((16, 128), jnp.float32))
            ys[level][f] = squeeze(2, pack, step)
            for way in range(2):
                exchange(level, 1, f, way).start()
            sums = edge_sums(lambda k: sum_lanes[k], len(wide))
            for way in range(2):
                cs[level][way] = packed(step, [(2 * f + j, sums[way][j]) for j in range(2)], cs[level][way])

        loop(x_stage)
        for yway in range(2):
            for zway in range(2):
                corner(level, yway, zway).start()
        if level > 0:
            ship(level - 1, cuts[1], cuts[2])
            fill(level - 1, me)
            own(level - 1).start()

        for yway in range(2):
            for zway in range(2):
                corner(level, yway, zway).wait_recv()

        def z_stage(f, level=level, step=step, live=live):
            old = planes(f, step, work)
            for way in range(2):
                exchange(level, 1, f, way).wait_recv()
                exchange(level, 2, f, way).wait_recv()
            hy = tuple(hy_ref[level, half] for half in range(2))
            edges = edge_lanes(step, spread(3, yr[level][0, f], step), spread(4, yr[level][1, f], step), range(len(old)))
            for way in range(2):
                edges += edge_lanes(step, cr[level][0, way], cr[level][1, way], [2 * f, 2 * f + 1])
            extra = product(halves(jnp.concatenate(edges, axis=0)), hy)
            if step > 1:
                extra = jnp.where((lax.broadcasted_iota(jnp.int32, extra.shape, 0) % step) == 0, extra, 0.0)
            extra = [extra[16 * i:16 * i + 16] for i in range(len(edges))]
            far = []
            for way in range(2):
                if step == 1:
                    far += [zr[level][way, f, 0], zr[level][way, f, 1]]
                else:
                    mixed = spread(5 + way, zr[level][way, f], step)
                    far += [mixed, pltpu.roll(mixed, 127, 1)]
            edge = [v + x for v, x in zip(far, extra[len(old):])]
            old = [o + x for o, x in zip(old, extra)]
            new = lift_layers(old, *edge)
            if step > 1:
                new = [jnp.where(live, n, o) for n, o in zip(new, old)]
            put(f, step, new)
            if level + 1 < LEVELS:
                send_x(level + 1, f, new[::2])

        loop(z_stage)

    def gather(k):
        return pltpu.make_async_remote_copy(
            src_ref=gs, dst_ref=gr.at[iz], send_sem=g_send.at[k], recv_sem=g_recv.at[k],
            device_id={"gz": lax.rem(iz + k, n_gz)}, device_id_type=MESH)

    for i in range(2):
        for f in range(n_f):
            for j in range(2):
                low_rows[16 * i + 2 * f + j:16 * i + 2 * f + j + 1, :] = work[f * bz + 8 * i, 8 * j:8 * j + 1, :]
        low_rows[16 * i + 2 * n_f:16 * i + 16, :] = jnp.zeros((16 - 2 * n_f, 128), jnp.float32)
    pick = jnp.where(lax.broadcasted_iota(jnp.int32, (128, 128), 0) ==
                     8 * lax.broadcasted_iota(jnp.int32, (128, 128), 1), jnp.float32(1.0), jnp.float32(0.0))
    gs[...] = jnp.dot(low_rows[...], pick, precision=lax.Precision.HIGHEST, preferred_element_type=jnp.float32)
    for k in range(1, n_gz):
        gather(k).start()
    gr[iz] = gs[...]

    last = len(PARTS) - 1
    ship(last, 1, groups)
    fill(last, me)
    own(last).start()

    for k in range(1, n_gz):
        gather(k).wait_recv()
    four = lift_whole([gr[g, 16 * i:16 * i + 16, :] for g in range(n_gz) for i in range(2)])
    four[::2] = lift_whole(four[::2])
    for z, tile in enumerate(four):
        for f in range(n_f):
            coarse_ref[f, z] = tile[2 * f:2 * f + 2, :16]

    def finish(k, carry):
        for part in range(len(PARTS)):
            route(part, k).wait()
        return carry

    lax.fori_loop(1, groups, finish, 0)
    for part in range(len(PARTS)):
        own(part).wait()

    def unpack(k, carry):
        for part, (first, count, stride) in enumerate(PARTS):
            for x in range(count):
                at = (first + stride * x) * 128
                received_ref[pl.ds(pl.multiple_of(8 * k, 8), 8), at:at + 128] = inbox[part][pl.ds(8 * k, 8), x, :]
        return carry

    lax.fori_loop(0, groups * capacity // 8, unpack, 0)
    for k in range(1, n_gz):
        gather(k).wait_send()

    def sent(f):
        for level in range(LEVELS):
            for kind in range(3):
                for way in range(2):
                    exchange(level, kind, f, way).wait_send()

    loop(sent)
    for level in range(LEVELS):
        for yway in range(2):
            for zway in range(2):
                corner(level, yway, zway).wait_send()


def source_table(writers, groups, capacity):
    count = writers.shape[0]
    place = jnp.arange(count, dtype=jnp.int32)
    same = (writers[:, None] == writers[None, :]) & (place[None, :] < place[:, None])
    targets = writers * capacity + jnp.sum(same.astype(jnp.int32), axis=1)
    slots = jnp.arange(groups * capacity, dtype=jnp.int32)
    hit = (targets[None, :] == slots[:, None]).astype(jnp.int32)
    return count - jnp.sum(hit * (count - place)[None, :], axis=1)


def body(fields, tile_writer):
    n_gx, n_gy, n_gz = lax.axis_size("gx"), lax.axis_size("gy"), lax.axis_size("gz")
    n_f, bz, bx, by = fields.shape
    count = n_f * bz
    groups = n_gx * n_gy
    capacity = max(2, 7 * count // (5 * groups) + 1)
    source = source_table(tile_writer.reshape(count), groups, capacity)
    f32 = jnp.float32
    steps = [1 << level for level in range(LEVELS)]
    tables = constant_tables()
    scratch = [pltpu.VMEM(a.shape, a.dtype) for a in (fields, *tables)]
    scratch += [pltpu.VMEM((count + 1, bx, by), f32), pltpu.VMEM((7, bx, by), f32), pltpu.SemaphoreType.DMA((6,))]
    scratch += [pltpu.VMEM((groups, capacity, p[1], by), f32) for p in PARTS]
    scratch += [pltpu.VMEM((groups * capacity, p[1], by), f32) for p in PARTS]
    scratch += [pltpu.VMEM((2, n_f, 2 * bz // s, by), f32) for s in steps] * 2
    scratch += [pltpu.VMEM((n_f, bx // s, by), f32) for s in steps]
    scratch += [pltpu.VMEM((2, n_f, bx // s, by), f32) for s in steps]
    scratch += [pltpu.VMEM((2, n_f, 2, bx, by) if s == 1 else (2, n_f, bx // s, by), f32) for s in steps] * 2
    scratch += [pltpu.VMEM((2, bx, by), f32) for s in steps] + [pltpu.VMEM((2, 2, bx, by), f32) for s in steps]
    scratch += [pltpu.VMEM((32, by), f32)] * 2 + [pltpu.VMEM((n_gz, 32, by), f32)]
    scratch += [pltpu.SemaphoreType.DMA((3 * LEVELS, 2, n_f))] * 2
    scratch += [pltpu.SemaphoreType.DMA((LEVELS, 2, 2))] * 2
    scratch += [pltpu.SemaphoreType.DMA((n_gz,))] * 2 + [pltpu.SemaphoreType.DMA((len(PARTS), groups))] * 2
    scratch += [pltpu.SemaphoreType.DMA((len(PARTS),))]
    return pl.pallas_call(
        functools.partial(kernel, (n_gx, n_gy, n_gz, n_f, bz, capacity)),
        out_shape=(jax.ShapeDtypeStruct((n_f, 2 * n_gz, 2, by // 8), f32),
                   jax.ShapeDtypeStruct((groups * capacity, bx * by), f32)),
        in_specs=[pl.BlockSpec(memory_space=pltpu.SMEM)] + [pl.BlockSpec(memory_space=pltpu.HBM)] * 6,
        out_specs=(pl.BlockSpec(memory_space=pltpu.VMEM), pl.BlockSpec(memory_space=pltpu.VMEM)),
        scratch_shapes=scratch,
        compiler_params=pltpu.CompilerParams(collective_id=0, has_side_effects=True,
                                             vmem_limit_bytes=60 * 1024 * 1024),
    )(source, fields, *tables)


def solution(mesh):
    return jax.shard_map(
        body,
        mesh=mesh,
        in_specs=(P(None, "gz", "gx", "gy"), P("gx", "gy", "gz", None)),
        out_specs=(P(None, None, "gx", "gy"), P(("gx", "gy"), "gz")),
        check_vma=False,
    )
```

```python
import functools

import jax
import jax.numpy as jnp
import numpy as np
from jax import lax
from jax.experimental import pallas as pl
from jax.experimental.pallas import tpu as pltpu
from jax.sharding import PartitionSpec as P

P1 = -1.586134342059924
U1 = -0.052980118572961
P2 = 0.882911075530934
U2 = 0.443506852043971
LOW = 1.0 / 1.149604398860241
HIGH = 1.149604398860241
LEVELS = 3
PARTS = ((1, 8, 2), (2, 4, 4), (0, 4, 4))


def lift_matrix(n, step):
    basis = np.eye(n + 4)
    v, (a, b, c, e) = basis[:n].copy(), basis[n:]
    v[::step] = np.stack(lift_layers(list(v[::step]), a, b, c, e))
    return v


def edge_matrix(n, step):
    below, above = edge_sums(lambda k: np.eye(n)[k * step], n // step)
    return np.stack(below + above)


def tiles_at_once(level):
    return min(8, 16 >> level)


def matrices(level):
    step, t = 1 << level, tiles_at_once(level)
    x_all, x_edge, y_all, y_edge = lift_matrix(16, step), edge_matrix(16, step), lift_matrix(128, step), edge_matrix(128, step)
    mx, hx, ex = np.zeros((128, 128)), np.zeros((128, 32)), np.zeros((32, 128))
    for i in range(t):
        rows = slice(16 * i, 16 * i + 16)
        mx[rows, rows] = x_all[:, :16]
        for way in range(2):
            edge = slice(2 * t * way + 2 * i, 2 * t * way + 2 * i + 2)
            hx[rows, edge] = x_all[:, 16 + 2 * way:18 + 2 * way]
            ex[edge, rows] = x_edge[2 * way:2 * way + 2]
    mq, hy = np.zeros((128, 256)), np.zeros((128, 128))
    mq[:, :128] = y_all[:, :128].T
    for sum_index, offset in enumerate((2, 0, 3, 4)):
        hy[offset * step] = y_all[:, 128 + sum_index]
        for group in range(16):
            mq[:, 128 + group // step * (8 * step) + group % step + offset * step] = y_edge[sum_index]
    return mx, hx, ex, mq, hy


def constant_tables():
    tables = []
    for kind in zip(*[matrices(level) for level in range(LEVELS)]):
        whole = np.stack(kind).astype(np.float32)
        high = whole.astype(jnp.bfloat16)
        low = (whole - high.astype(np.float32)).astype(jnp.bfloat16)
        tables.append(jnp.asarray(np.stack([high, low], axis=1)))
    return tables


def halves(v):
    high = v.astype(jnp.bfloat16)
    return high, (v - high.astype(jnp.float32)).astype(jnp.bfloat16)


def product(a, b):
    dot = lambda p, q: jnp.dot(p, q, preferred_element_type=jnp.float32)
    return dot(a[0], b[0]) + dot(a[1], b[0]) + dot(a[0], b[1])


def edge_sums(get, n):
    a = get(n - 1) + P1 * get(n - 2)
    before = get(n - 3) + P1 * (get(n - 4) + get(n - 2))
    b = get(n - 2) + U1 * before
    c = get(0)
    after = get(1) + P1 * (c + get(2))
    e = c + U1 * after
    return (a, b), (c, e)


def lift_layers(v, a, b, c, e):
    s, d = list(v[0::2]), list(v[1::2])
    n = len(s)
    s_end = [c]
    d = [d[i] + P1 * (s[i] + (s + s_end)[i + 1]) for i in range(n)]
    dm = a + P1 * s[0]
    sm = b + U1 * dm
    s_top = e + U1 * d[-1]
    s = [s[i] + U1 * (([dm] + d)[i] + d[i]) for i in range(n)]
    d = [d[i] + P2 * (s[i] + (s + [s_top])[i + 1]) for i in range(n)]
    dm = dm + P2 * (sm + s[0])
    s = [s[i] + U2 * (([dm] + d)[i] + d[i]) for i in range(n)]
    out = []
    for i in range(n):
        out += [s[i] * LOW, d[i] * HIGH]
    return out


def lift_whole(v):
    s, d = list(v[0::2]), list(v[1::2])
    n = len(s)
    d = [d[i] + P1 * (s[i] + s[(i + 1) % n]) for i in range(n)]
    s = [s[i] + U1 * (d[i - 1] + d[i]) for i in range(n)]
    d = [d[i] + P2 * (s[i] + s[(i + 1) % n]) for i in range(n)]
    s = [s[i] + U2 * (d[i - 1] + d[i]) for i in range(n)]
    out = []
    for i in range(n):
        out += [s[i] * LOW, d[i] * HIGH]
    return out


def kernel(sizes, source_ref, *refs):
    n_gx, n_gy, n_gz, n_f, bz, capacity = sizes
    given, coarse_ref, inbox, held, scratch = refs[:6], refs[6], refs[7:10], refs[10:16], refs[16:]
    fields_ref, mx_ref, hx_ref, ex_ref, mq_ref, hy_ref = held
    work, turn_rows, load_sem = scratch[:3]
    outbox, scratch = scratch[3:6], scratch[6:]
    loads = [pltpu.make_async_copy(a, b, load_sem.at[i]) for i, (a, b) in enumerate(zip(given, held))]
    for load in loads:
        load.start()
    xs, xr, ys, yr, zs, zr, cs, cr = [scratch[LEVELS * i:LEVELS * (i + 1)] for i in range(8)]
    low_rows, gs, gr, send, recv, c_send, c_recv, g_send, g_recv, a_send, a_recv, own_sem = scratch[8 * LEVELS:]
    groups = n_gx * n_gy
    ix, iy, iz = lax.axis_index("gx"), lax.axis_index("gy"), lax.axis_index("gz")
    me = ix * n_gy + iy
    place = {"gx": (ix, n_gx), "gy": (iy, n_gy), "gz": (iz, n_gz)}
    MESH = pl.DeviceIdType.MESH

    def beside(axis, way):
        index, count = place[axis]
        return lax.rem(index + (1 if way == 0 else count - 1), count)

    barrier = pltpu.get_barrier_semaphore()

    def greet_plane(k, carry):
        w = lax.rem(me + k, groups)
        pl.semaphore_signal(barrier, inc=1, device_id={"gx": w // n_gy, "gy": lax.rem(w, n_gy)},
                            device_id_type=MESH)
        return carry

    lax.fori_loop(1, groups, greet_plane, 0)
    for k in range(1, n_gz):
        pl.semaphore_signal(barrier, inc=1, device_id={"gz": lax.rem(iz + k, n_gz)}, device_id_type=MESH)
    for yway in range(2):
        for zway in range(2):
            pl.semaphore_signal(barrier, inc=1, device_id={"gy": beside("gy", yway), "gz": beside("gz", zway)},
                                device_id_type=MESH)
    for load in loads:
        load.wait()
    pl.semaphore_wait(barrier, groups - 1 + n_gz - 1 + 4)

    def exchange(level, kind, f, way):
        axis = ("gx", "gy", "gz")[kind]
        out, into = ((xs, xr), (ys, yr), (zs, zr))[kind]
        src = out[level].at[f] if kind == 1 else out[level].at[way, f]
        row = level * 3 + kind
        return pltpu.make_async_remote_copy(
            src_ref=src, dst_ref=into[level].at[way, f],
            send_sem=send.at[row, way, f], recv_sem=recv.at[row, way, f],
            device_id={axis: beside(axis, way)}, device_id_type=MESH)

    def corner(level, yway, zway):
        return pltpu.make_async_remote_copy(
            src_ref=cs[level].at[zway], dst_ref=cr[level].at[yway, zway],
            send_sem=c_send.at[level, yway, zway], recv_sem=c_recv.at[level, yway, zway],
            device_id={"gy": beside("gy", yway), "gz": beside("gz", zway)}, device_id_type=MESH)

    row = lax.broadcasted_iota(jnp.int32, (16, 128), 0)
    lane = lax.broadcasted_iota(jnp.int32, (16, 128), 1)

    def send_x(level, f, tiles):
        t = tiles_at_once(level)
        sums = tuple(ex_ref[level, half, :4 * t, :16 * t] for half in range(2))
        for k in range(0, len(tiles), t):
            edge = product(sums, halves(jnp.concatenate(tiles[k:k + t], axis=0)))
            for way in range(2):
                xs[level][way, f, 2 * k:2 * (k + t), :] = edge[2 * t * way:2 * t * (way + 1)]
        for way in range(2):
            exchange(level, 0, f, way).start()

    def spot(i, step):
        return i // step * (8 * step) + i % step

    def packed(step, pairs, pack):
        for i, v in pairs:
            start = i // step * (8 * step)
            here = (lane >= start) & (lane < start + 8 * step) & (lane % step == i % step)
            pack = jnp.where(here, v, pack)
        return pack

    def edge_lanes(step, below, above, spots):
        both = jnp.where(lane % (8 * step) // step < 3, below, above)
        return [pltpu.roll(both, (128 - spot(i, step)) % 128, 1) for i in spots]

    def planes(f, step, ref):
        return [ref[f * bz + z] if ref is work else ref[f, z] for z in range(0, bz, step)]

    def put(f, step, tiles):
        for i, tile in enumerate(tiles):
            work[f * bz + i * step] = tile

    def loop(body):
        def run(f, carry):
            body(f)
            return carry
        lax.fori_loop(0, n_f, run, 0)

    def squeeze(slot, v, step):
        if step == 1:
            return v
        turn_rows[slot] = v
        return turn_rows[slot, pl.ds(0, 16 // step, step), :]

    def spread(slot, v, step):
        if step == 1:
            return v
        turn_rows[slot, pl.ds(0, 16 // step, step), :] = v
        return turn_rows[slot]

    def route(part, k):
        w = lax.rem(me + k, groups)
        return pltpu.make_async_remote_copy(
            src_ref=outbox[part].at[w], dst_ref=inbox[part].at[pl.ds(me * capacity, capacity)],
            send_sem=a_send.at[part, k], recv_sem=a_recv.at[part, k],
            device_id={"gx": w // n_gy, "gy": lax.rem(w, n_gy)}, device_id_type=MESH)

    def own(part):
        return pltpu.make_async_copy(
            outbox[part].at[me], inbox[part].at[pl.ds(me * capacity, capacity)], own_sem.at[part])

    def fill(part, w):
        first, count, stride = PARTS[part]
        for r in range(capacity):
            outbox[part][w, r] = work[source_ref[w * capacity + r], pl.ds(first, count, stride), :]

    def ship(part, first, last):
        def run(k, carry):
            fill(part, lax.rem(me + k, groups))
            route(part, k).start()
            return carry
        lax.fori_loop(first, last, run, 0)

    cuts = [1 + (groups - 1) * i // 2 for i in range(3)]
    turn_rows[...] = jnp.zeros_like(turn_rows)
    work[n_f * bz] = jnp.zeros((16, 128), jnp.float32)
    loop(lambda f: send_x(0, f, planes(f, 1, fields_ref)))
    for level in range(LEVELS):
        step = 1 << level
        if level > 0:
            ship(level - 1, cuts[0], cuts[1])
        for zway in range(2):
            cs[level][zway] = jnp.zeros((16, 128), jnp.float32)

        t = tiles_at_once(level)
        live = (row % step == 0) & (lane % step == 0)

        def x_stage(f, level=level, step=step, t=t, live=live):
            tiles = planes(f, step, fields_ref if level == 0 else work)
            for way in range(2):
                exchange(level, 0, f, way).wait_recv()
            mx = tuple(mx_ref[level, half, :16 * t, :16 * t] for half in range(2))
            hx = tuple(hx_ref[level, half, :16 * t, :4 * t] for half in range(2))
            mq = tuple(mq_ref[level, half] for half in range(2))
            wide = []
            for k in range(0, len(tiles), t):
                edge = jnp.concatenate([xr[level][way, f, 2 * k:2 * (k + t), :] for way in range(2)], axis=0)
                lifted = product(mx, halves(jnp.concatenate(tiles[k:k + t], axis=0))) + product(hx, halves(edge))
                lifted = product(halves(lifted), mq)
                wide += [lifted[16 * i:16 * i + 16] for i in range(t)]
            own_lanes, sum_lanes = [w[:, :128] for w in wide], [w[:, 128:] for w in wide]
            put(f, step, own_lanes if step == 1 else [jnp.where(live, n, o) for n, o in zip(own_lanes, tiles)])
            sums = edge_sums(lambda k: own_lanes[k], len(wide))
            for way in range(2):
                if step == 1:
                    for j in range(2):
                        zs[level][way, f, j] = sums[way][j]
                else:
                    mixed = jnp.where(lane % step == 0, sums[way][0], pltpu.roll(sums[way][1], 1, 1))
                    zs[level][way, f] = squeeze(way, mixed, step)
                exchange(level, 2, f, way).start()
            pack = packed(step, list(enumerate(sum_lanes)), jnp.zeros((16, 128), jnp.float32))
            ys[level][f] = squeeze(2, pack, step)
            for way in range(2):
                exchange(level, 1, f, way).start()
            sums = edge_sums(lambda k: sum_lanes[k], len(wide))
            for way in range(2):
                cs[level][way] = packed(step, [(2 * f + j, sums[way][j]) for j in range(2)], cs[level][way])

        loop(x_stage)
        for yway in range(2):
            for zway in range(2):
                corner(level, yway, zway).start()
        if level > 0:
            ship(level - 1, cuts[1], cuts[2])
            fill(level - 1, me)
            own(level - 1).start()

        for yway in range(2):
            for zway in range(2):
                corner(level, yway, zway).wait_recv()

        def z_stage(f, level=level, step=step, live=live):
            old = planes(f, step, work)
            for way in range(2):
                exchange(level, 1, f, way).wait_recv()
                exchange(level, 2, f, way).wait_recv()
            hy = tuple(hy_ref[level, half] for half in range(2))
            edges = edge_lanes(step, spread(3, yr[level][0, f], step), spread(4, yr[level][1, f], step), range(len(old)))
            for way in range(2):
                edges += edge_lanes(step, cr[level][0, way], cr[level][1, way], [2 * f, 2 * f + 1])
            extra = product(halves(jnp.concatenate(edges, axis=0)), hy)
            if step > 1:
                extra = jnp.where((lax.broadcasted_iota(jnp.int32, extra.shape, 0) % step) == 0, extra, 0.0)
            extra = [extra[16 * i:16 * i + 16] for i in range(len(edges))]
            far = []
            for way in range(2):
                if step == 1:
                    far += [zr[level][way, f, 0], zr[level][way, f, 1]]
                else:
                    mixed = spread(5 + way, zr[level][way, f], step)
                    far += [mixed, pltpu.roll(mixed, 127, 1)]
            edge = [v + x for v, x in zip(far, extra[len(old):])]
            old = [o + x for o, x in zip(old, extra)]
            new = lift_layers(old, *edge)
            if step > 1:
                new = [jnp.where(live, n, o) for n, o in zip(new, old)]
            put(f, step, new)
            if level + 1 < LEVELS:
                send_x(level + 1, f, new[::2])

        loop(z_stage)

    def gather(k):
        return pltpu.make_async_remote_copy(
            src_ref=gs, dst_ref=gr.at[iz], send_sem=g_send.at[k], recv_sem=g_recv.at[k],
            device_id={"gz": lax.rem(iz + k, n_gz)}, device_id_type=MESH)

    for i in range(2):
        for f in range(n_f):
            for j in range(2):
                low_rows[16 * i + 2 * f + j:16 * i + 2 * f + j + 1, :] = work[f * bz + 8 * i, 8 * j:8 * j + 1, :]
        low_rows[16 * i + 2 * n_f:16 * i + 16, :] = jnp.zeros((16 - 2 * n_f, 128), jnp.float32)
    pick = jnp.where(lax.broadcasted_iota(jnp.int32, (128, 128), 0) ==
                     8 * lax.broadcasted_iota(jnp.int32, (128, 128), 1), jnp.float32(1.0), jnp.float32(0.0))
    gs[...] = jnp.dot(low_rows[...], pick, precision=lax.Precision.HIGHEST, preferred_element_type=jnp.float32)
    for k in range(1, n_gz):
        gather(k).start()
    gr[iz] = gs[...]

    last = len(PARTS) - 1
    ship(last, 1, groups)
    fill(last, me)
    own(last).start()

    for k in range(1, n_gz):
        gather(k).wait_recv()
    four = lift_whole([gr[g, 16 * i:16 * i + 16, :] for g in range(n_gz) for i in range(2)])
    four[::2] = lift_whole(four[::2])
    for z, tile in enumerate(four):
        for f in range(n_f):
            coarse_ref[f, z] = tile[2 * f:2 * f + 2, :16]

    def finish(k, carry):
        for part in range(len(PARTS)):
            route(part, k).wait()
        return carry

    lax.fori_loop(1, groups, finish, 0)
    for part in range(len(PARTS)):
        own(part).wait()

    for k in range(1, n_gz):
        gather(k).wait_send()

    def sent(f):
        for level in range(LEVELS):
            for kind in range(3):
                for way in range(2):
                    exchange(level, kind, f, way).wait_send()

    loop(sent)
    for level in range(LEVELS):
        for yway in range(2):
            for zway in range(2):
                corner(level, yway, zway).wait_send()


def lay_out(coarse_ref, *refs):
    inbox, (bands_ref, received_ref) = refs[:len(PARTS)], refs[len(PARTS):]
    bands_ref[...] = coarse_ref[...]

    def unpack(k, carry):
        rows = pl.ds(pl.multiple_of(8 * k, 8), 8)
        for part, (first, count, stride) in enumerate(PARTS):
            for x in range(count):
                at = (first + stride * x) * 128
                received_ref[rows, at:at + 128] = inbox[part][rows, x, :]
        return carry

    lax.fori_loop(0, received_ref.shape[0] // 8, unpack, 0)


def source_table(writers, groups, capacity):
    count = writers.shape[0]
    place = jnp.arange(count, dtype=jnp.int32)
    same = (writers[:, None] == writers[None, :]) & (place[None, :] < place[:, None])
    targets = writers * capacity + jnp.sum(same.astype(jnp.int32), axis=1)
    slots = jnp.arange(groups * capacity, dtype=jnp.int32)
    hit = (targets[None, :] == slots[:, None]).astype(jnp.int32)
    return count - jnp.sum(hit * (count - place)[None, :], axis=1)


def body(fields, tile_writer):
    n_gx, n_gy, n_gz = lax.axis_size("gx"), lax.axis_size("gy"), lax.axis_size("gz")
    n_f, bz, bx, by = fields.shape
    count = n_f * bz
    groups = n_gx * n_gy
    capacity = max(2, 7 * count // (5 * groups) + 1)
    source = source_table(tile_writer.reshape(count), groups, capacity)
    f32 = jnp.float32
    steps = [1 << level for level in range(LEVELS)]
    tables = constant_tables()
    scratch = [pltpu.VMEM(a.shape, a.dtype) for a in (fields, *tables)]
    scratch += [pltpu.VMEM((count + 1, bx, by), f32), pltpu.VMEM((7, bx, by), f32), pltpu.SemaphoreType.DMA((6,))]
    scratch += [pltpu.VMEM((groups, capacity, p[1], by), f32) for p in PARTS]
    scratch += [pltpu.VMEM((2, n_f, 2 * bz // s, by), f32) for s in steps] * 2
    scratch += [pltpu.VMEM((n_f, bx // s, by), f32) for s in steps]
    scratch += [pltpu.VMEM((2, n_f, bx // s, by), f32) for s in steps]
    scratch += [pltpu.VMEM((2, n_f, 2, bx, by) if s == 1 else (2, n_f, bx // s, by), f32) for s in steps] * 2
    scratch += [pltpu.VMEM((2, bx, by), f32) for s in steps] + [pltpu.VMEM((2, 2, bx, by), f32) for s in steps]
    scratch += [pltpu.VMEM((32, by), f32)] * 2 + [pltpu.VMEM((n_gz, 32, by), f32)]
    scratch += [pltpu.SemaphoreType.DMA((3 * LEVELS, 2, n_f))] * 2
    scratch += [pltpu.SemaphoreType.DMA((LEVELS, 2, 2))] * 2
    scratch += [pltpu.SemaphoreType.DMA((n_gz,))] * 2 + [pltpu.SemaphoreType.DMA((len(PARTS), groups))] * 2
    scratch += [pltpu.SemaphoreType.DMA((len(PARTS),))]
    coarse, *inbox = pl.pallas_call(
        functools.partial(kernel, (n_gx, n_gy, n_gz, n_f, bz, capacity)),
        out_shape=(jax.ShapeDtypeStruct((n_f, 2 * n_gz, 2, by // 8), f32),
                   *[jax.ShapeDtypeStruct((groups * capacity, p[1], by), f32) for p in PARTS]),
        in_specs=[pl.BlockSpec(memory_space=pltpu.SMEM)] + [pl.BlockSpec(memory_space=pltpu.HBM)] * 6,
        out_specs=(pl.BlockSpec(memory_space=pltpu.VMEM), *[pl.BlockSpec(memory_space=pltpu.HBM)] * len(PARTS)),
        scratch_shapes=scratch,
        compiler_params=pltpu.CompilerParams(collective_id=0, has_side_effects=True,
                                             vmem_limit_bytes=60 * 1024 * 1024),
    )(source, fields, *tables)
    rows = groups * capacity
    block = 40 if rows % 40 == 0 else 64
    bands = pl.BlockSpec(coarse.shape, lambda i: (0, 0, 0, 0))
    return pl.pallas_call(
        lay_out,
        grid=(rows // block,),
        out_shape=(jax.ShapeDtypeStruct(coarse.shape, f32), jax.ShapeDtypeStruct((rows, bx * by), f32)),
        in_specs=[bands] + [pl.BlockSpec((block, p[1], by), lambda i: (i, 0, 0)) for p in PARTS],
        out_specs=(bands, pl.BlockSpec((block, bx * by), lambda i: (i, 0))),
        compiler_params=pltpu.CompilerParams(vmem_limit_bytes=60 * 1024 * 1024),
    )(coarse, *inbox)


def solution(mesh):
    return jax.shard_map(
        body,
        mesh=mesh,
        in_specs=(P(None, "gz", "gx", "gy"), P("gx", "gy", "gz", None)),
        out_specs=(P(None, None, "gx", "gy"), P(("gx", "gy"), "gz")),
        check_vma=False,
    )
```

```python
import functools

import jax
import jax.numpy as jnp
import numpy as np
from jax import lax
from jax.experimental import pallas as pl
from jax.experimental.pallas import tpu as pltpu
from jax.sharding import PartitionSpec as P

P1 = -1.586134342059924
U1 = -0.052980118572961
P2 = 0.882911075530934
U2 = 0.443506852043971
LOW = 1.0 / 1.149604398860241
HIGH = 1.149604398860241
LEVELS = 3
PARTS = ((1, 8, 2), (2, 4, 4), (0, 4, 4))


def lift_matrix(n, step):
    basis = np.eye(n + 4)
    v, (a, b, c, e) = basis[:n].copy(), basis[n:]
    v[::step] = np.stack(lift_layers(list(v[::step]), a, b, c, e))
    return v


def edge_matrix(n, step):
    below, above = edge_sums(lambda k: np.eye(n)[k * step], n // step)
    return np.stack(below + above)


def tiles_at_once(level):
    return min(8, 16 >> level)


def matrices(level):
    step, t = 1 << level, tiles_at_once(level)
    x_all, x_edge, y_all, y_edge = lift_matrix(16, step), edge_matrix(16, step), lift_matrix(128, step), edge_matrix(128, step)
    mx, hx, ex = np.zeros((128, 128)), np.zeros((128, 32)), np.zeros((32, 128))
    for i in range(t):
        rows = slice(16 * i, 16 * i + 16)
        mx[rows, rows] = x_all[:, :16]
        for way in range(2):
            edge = slice(2 * t * way + 2 * i, 2 * t * way + 2 * i + 2)
            hx[rows, edge] = x_all[:, 16 + 2 * way:18 + 2 * way]
            ex[edge, rows] = x_edge[2 * way:2 * way + 2]
    mq, hy = np.zeros((128, 256)), np.zeros((128, 128))
    mq[:, :128] = y_all[:, :128].T
    for sum_index, offset in enumerate((2, 0, 3, 4)):
        hy[offset * step] = y_all[:, 128 + sum_index]
        for group in range(16):
            mq[:, 128 + group // step * (8 * step) + group % step + offset * step] = y_edge[sum_index]
    return mx, hx, ex, mq, hy


def constant_tables():
    tables = []
    for kind in zip(*[matrices(level) for level in range(LEVELS)]):
        whole = np.stack(kind).astype(np.float32)
        high = whole.astype(jnp.bfloat16)
        low = (whole - high.astype(np.float32)).astype(jnp.bfloat16)
        tables.append(jnp.asarray(np.stack([high, low], axis=1)))
    return tables


def halves(v):
    high = v.astype(jnp.bfloat16)
    return high, (v - high.astype(jnp.float32)).astype(jnp.bfloat16)


def product(a, b):
    dot = lambda p, q: jnp.dot(p, q, preferred_element_type=jnp.float32)
    return dot(a[0], b[0]) + dot(a[1], b[0]) + dot(a[0], b[1])


def edge_sums(get, n):
    a = get(n - 1) + P1 * get(n - 2)
    before = get(n - 3) + P1 * (get(n - 4) + get(n - 2))
    b = get(n - 2) + U1 * before
    c = get(0)
    after = get(1) + P1 * (c + get(2))
    e = c + U1 * after
    return (a, b), (c, e)


def lift_layers(v, a, b, c, e):
    s, d = list(v[0::2]), list(v[1::2])
    n = len(s)
    s_end = [c]
    d = [d[i] + P1 * (s[i] + (s + s_end)[i + 1]) for i in range(n)]
    dm = a + P1 * s[0]
    sm = b + U1 * dm
    s_top = e + U1 * d[-1]
    s = [s[i] + U1 * (([dm] + d)[i] + d[i]) for i in range(n)]
    d = [d[i] + P2 * (s[i] + (s + [s_top])[i + 1]) for i in range(n)]
    dm = dm + P2 * (sm + s[0])
    s = [s[i] + U2 * (([dm] + d)[i] + d[i]) for i in range(n)]
    out = []
    for i in range(n):
        out += [s[i] * LOW, d[i] * HIGH]
    return out


def lift_whole(v):
    s, d = list(v[0::2]), list(v[1::2])
    n = len(s)
    d = [d[i] + P1 * (s[i] + s[(i + 1) % n]) for i in range(n)]
    s = [s[i] + U1 * (d[i - 1] + d[i]) for i in range(n)]
    d = [d[i] + P2 * (s[i] + s[(i + 1) % n]) for i in range(n)]
    s = [s[i] + U2 * (d[i - 1] + d[i]) for i in range(n)]
    out = []
    for i in range(n):
        out += [s[i] * LOW, d[i] * HIGH]
    return out


def kernel(sizes, source_ref, *refs):
    n_gx, n_gy, n_gz, n_f, bz, capacity = sizes
    given, coarse_ref, inbox, held, scratch = refs[:6], refs[6], refs[7:10], refs[10:16], refs[16:]
    fields_ref, mx_ref, hx_ref, ex_ref, mq_ref, hy_ref = held
    work, turn_rows, load_sem = scratch[:3]
    outbox, scratch = scratch[3:6], scratch[6:]
    loads = [pltpu.make_async_copy(a, b, load_sem.at[i]) for i, (a, b) in enumerate(zip(given, held))]
    for load in loads:
        load.start()
    xs, xr, ys, yr, zs, zr, cs, cr = [scratch[LEVELS * i:LEVELS * (i + 1)] for i in range(8)]
    low_rows, gs, gr, send, recv, c_send, c_recv, g_send, g_recv, a_send, a_recv, own_sem = scratch[8 * LEVELS:]
    groups = n_gx * n_gy
    ix, iy, iz = lax.axis_index("gx"), lax.axis_index("gy"), lax.axis_index("gz")
    me = ix * n_gy + iy
    place = {"gx": (ix, n_gx), "gy": (iy, n_gy), "gz": (iz, n_gz)}
    MESH = pl.DeviceIdType.MESH

    def beside(axis, way):
        index, count = place[axis]
        return lax.rem(index + (1 if way == 0 else count - 1), count)

    barrier = pltpu.get_barrier_semaphore()

    def greet_plane(k, carry):
        w = lax.rem(me + k, groups)
        pl.semaphore_signal(barrier, inc=1, device_id={"gx": w // n_gy, "gy": lax.rem(w, n_gy)},
                            device_id_type=MESH)
        return carry

    lax.fori_loop(1, groups, greet_plane, 0)
    for k in range(1, n_gz):
        pl.semaphore_signal(barrier, inc=1, device_id={"gz": lax.rem(iz + k, n_gz)}, device_id_type=MESH)
    for yway in range(2):
        for zway in range(2):
            pl.semaphore_signal(barrier, inc=1, device_id={"gy": beside("gy", yway), "gz": beside("gz", zway)},
                                device_id_type=MESH)
    for load in loads:
        load.wait()
    pl.semaphore_wait(barrier, groups - 1 + n_gz - 1 + 4)

    def exchange(level, kind, f, way):
        axis = ("gx", "gy", "gz")[kind]
        out, into = ((xs, xr), (ys, yr), (zs, zr))[kind]
        src = out[level].at[f] if kind == 1 else out[level].at[way, f]
        row = level * 3 + kind
        return pltpu.make_async_remote_copy(
            src_ref=src, dst_ref=into[level].at[way, f],
            send_sem=send.at[row, way, f], recv_sem=recv.at[row, way, f],
            device_id={axis: beside(axis, way)}, device_id_type=MESH)

    def corner(level, yway, zway):
        return pltpu.make_async_remote_copy(
            src_ref=cs[level].at[zway], dst_ref=cr[level].at[yway, zway],
            send_sem=c_send.at[level, yway, zway], recv_sem=c_recv.at[level, yway, zway],
            device_id={"gy": beside("gy", yway), "gz": beside("gz", zway)}, device_id_type=MESH)

    row = lax.broadcasted_iota(jnp.int32, (16, 128), 0)
    lane = lax.broadcasted_iota(jnp.int32, (16, 128), 1)

    def send_x(level, f, tiles):
        t = tiles_at_once(level)
        sums = tuple(ex_ref[level, half, :4 * t, :16 * t] for half in range(2))
        for k in range(0, len(tiles), t):
            edge = product(sums, halves(jnp.concatenate(tiles[k:k + t], axis=0)))
            for way in range(2):
                xs[level][way, f, 2 * k:2 * (k + t), :] = edge[2 * t * way:2 * t * (way + 1)]
        for way in range(2):
            exchange(level, 0, f, way).start()

    def spot(i, step):
        return i // step * (8 * step) + i % step

    def packed(step, pairs, pack):
        for i, v in pairs:
            start = i // step * (8 * step)
            here = (lane >= start) & (lane < start + 8 * step) & (lane % step == i % step)
            pack = jnp.where(here, v, pack)
        return pack

    def edge_lanes(step, below, above, spots):
        both = jnp.where(lane % (8 * step) // step < 3, below, above)
        return [pltpu.roll(both, (128 - spot(i, step)) % 128, 1) for i in spots]

    def planes(f, step, ref):
        return [ref[f * bz + z] if ref is work else ref[f, z] for z in range(0, bz, step)]

    def put(f, step, tiles):
        for i, tile in enumerate(tiles):
            work[f * bz + i * step] = tile

    def loop(body):
        def run(f, carry):
            body(f)
            return carry
        lax.fori_loop(0, n_f, run, 0)

    def squeeze(slot, v, step):
        if step == 1:
            return v
        turn_rows[slot] = v
        return turn_rows[slot, pl.ds(0, 16 // step, step), :]

    def spread(slot, v, step):
        if step == 1:
            return v
        turn_rows[slot, pl.ds(0, 16 // step, step), :] = v
        return turn_rows[slot]

    def route(part, k):
        w = lax.rem(me + k, groups)
        return pltpu.make_async_remote_copy(
            src_ref=outbox[part].at[w], dst_ref=inbox[part].at[pl.ds(me * capacity, capacity)],
            send_sem=a_send.at[part, k], recv_sem=a_recv.at[part, k],
            device_id={"gx": w // n_gy, "gy": lax.rem(w, n_gy)}, device_id_type=MESH)

    def own(part):
        return pltpu.make_async_copy(
            outbox[part].at[me], inbox[part].at[pl.ds(me * capacity, capacity)], own_sem.at[part])

    def fill(part, w):
        first, count, stride = PARTS[part]
        for r in range(capacity):
            outbox[part][w, r] = work[source_ref[w * capacity + r], pl.ds(first, count, stride), :]

    def ship(part, first, last):
        def run(k, carry):
            fill(part, lax.rem(me + k, groups))
            route(part, k).start()
            return carry
        lax.fori_loop(first, last, run, 0)

    cuts = [1 + (groups - 1) * i // 2 for i in range(3)]
    turn_rows[...] = jnp.zeros_like(turn_rows)
    work[n_f * bz] = jnp.zeros((16, 128), jnp.float32)
    loop(lambda f: send_x(0, f, planes(f, 1, fields_ref)))
    for level in range(LEVELS):
        step = 1 << level
        if level > 0:
            ship(level - 1, cuts[0], cuts[1])
        for zway in range(2):
            cs[level][zway] = jnp.zeros((16, 128), jnp.float32)

        t = tiles_at_once(level)
        live = (row % step == 0) & (lane % step == 0)

        def x_stage(f, level=level, step=step, t=t, live=live):
            tiles = planes(f, step, fields_ref if level == 0 else work)
            for way in range(2):
                exchange(level, 0, f, way).wait_recv()
            mx = tuple(mx_ref[level, half, :16 * t, :16 * t] for half in range(2))
            hx = tuple(hx_ref[level, half, :16 * t, :4 * t] for half in range(2))
            mq = tuple(mq_ref[level, half] for half in range(2))
            wide = []
            for k in range(0, len(tiles), t):
                edge = jnp.concatenate([xr[level][way, f, 2 * k:2 * (k + t), :] for way in range(2)], axis=0)
                lifted = product(mx, halves(jnp.concatenate(tiles[k:k + t], axis=0))) + product(hx, halves(edge))
                lifted = product(halves(lifted), mq)
                wide += [lifted[16 * i:16 * i + 16] for i in range(t)]
            own_lanes, sum_lanes = [w[:, :128] for w in wide], [w[:, 128:] for w in wide]
            put(f, step, own_lanes if step == 1 else [jnp.where(live, n, o) for n, o in zip(own_lanes, tiles)])
            sums = edge_sums(lambda k: own_lanes[k], len(wide))
            for way in range(2):
                if step == 1:
                    for j in range(2):
                        zs[level][way, f, j] = sums[way][j]
                else:
                    mixed = jnp.where(lane % step == 0, sums[way][0], pltpu.roll(sums[way][1], 1, 1))
                    zs[level][way, f] = squeeze(way, mixed, step)
                exchange(level, 2, f, way).start()
            pack = packed(step, list(enumerate(sum_lanes)), jnp.zeros((16, 128), jnp.float32))
            ys[level][f] = squeeze(2, pack, step)
            for way in range(2):
                exchange(level, 1, f, way).start()
            sums = edge_sums(lambda k: sum_lanes[k], len(wide))
            for way in range(2):
                cs[level][way] = packed(step, [(2 * f + j, sums[way][j]) for j in range(2)], cs[level][way])

        loop(x_stage)
        for yway in range(2):
            for zway in range(2):
                corner(level, yway, zway).start()
        if level > 0:
            ship(level - 1, cuts[1], cuts[2])
            fill(level - 1, me)
            own(level - 1).start()

        for yway in range(2):
            for zway in range(2):
                corner(level, yway, zway).wait_recv()

        def z_stage(f, level=level, step=step, live=live):
            old = planes(f, step, work)
            for way in range(2):
                exchange(level, 1, f, way).wait_recv()
                exchange(level, 2, f, way).wait_recv()
            hy = tuple(hy_ref[level, half] for half in range(2))
            edges = edge_lanes(step, spread(3, yr[level][0, f], step), spread(4, yr[level][1, f], step), range(len(old)))
            for way in range(2):
                edges += edge_lanes(step, cr[level][0, way], cr[level][1, way], [2 * f, 2 * f + 1])
            extra = product(halves(jnp.concatenate(edges, axis=0)), hy)
            if step > 1:
                extra = jnp.where((lax.broadcasted_iota(jnp.int32, extra.shape, 0) % step) == 0, extra, 0.0)
            extra = [extra[16 * i:16 * i + 16] for i in range(len(edges))]
            far = []
            for way in range(2):
                if step == 1:
                    far += [zr[level][way, f, 0], zr[level][way, f, 1]]
                else:
                    mixed = spread(5 + way, zr[level][way, f], step)
                    far += [mixed, pltpu.roll(mixed, 127, 1)]
            edge = [v + x for v, x in zip(far, extra[len(old):])]
            old = [o + x for o, x in zip(old, extra)]
            new = lift_layers(old, *edge)
            if step > 1:
                new = [jnp.where(live, n, o) for n, o in zip(new, old)]
            put(f, step, new)
            if level + 1 < LEVELS:
                send_x(level + 1, f, new[::2])

        loop(z_stage)

    def gather(k):
        return pltpu.make_async_remote_copy(
            src_ref=gs, dst_ref=gr.at[iz], send_sem=g_send.at[k], recv_sem=g_recv.at[k],
            device_id={"gz": lax.rem(iz + k, n_gz)}, device_id_type=MESH)

    for i in range(2):
        for f in range(n_f):
            for j in range(2):
                low_rows[16 * i + 2 * f + j:16 * i + 2 * f + j + 1, :] = work[f * bz + 8 * i, 8 * j:8 * j + 1, :]
        low_rows[16 * i + 2 * n_f:16 * i + 16, :] = jnp.zeros((16 - 2 * n_f, 128), jnp.float32)
    pick = jnp.where(lax.broadcasted_iota(jnp.int32, (128, 128), 0) ==
                     8 * lax.broadcasted_iota(jnp.int32, (128, 128), 1), jnp.float32(1.0), jnp.float32(0.0))
    gs[...] = jnp.dot(low_rows[...], pick, precision=lax.Precision.HIGHEST, preferred_element_type=jnp.float32)
    for k in range(1, n_gz):
        gather(k).start()
    gr[iz] = gs[...]

    last = len(PARTS) - 1
    ship(last, 1, groups)
    fill(last, me)
    own(last).start()

    for k in range(1, n_gz):
        gather(k).wait_recv()
    four = lift_whole([gr[g, 16 * i:16 * i + 16, :] for g in range(n_gz) for i in range(2)])
    four[::2] = lift_whole(four[::2])
    for z, tile in enumerate(four):
        for f in range(n_f):
            coarse_ref[f, z] = tile[2 * f:2 * f + 2, :16]

    def finish(k, carry):
        for part in range(len(PARTS)):
            route(part, k).wait()
        return carry

    lax.fori_loop(1, groups, finish, 0)
    for part in range(len(PARTS)):
        own(part).wait()

    for k in range(1, n_gz):
        gather(k).wait_send()

    def sent(f):
        for level in range(LEVELS):
            for kind in range(3):
                for way in range(2):
                    exchange(level, kind, f, way).wait_send()

    loop(sent)
    for level in range(LEVELS):
        for yway in range(2):
            for zway in range(2):
                corner(level, yway, zway).wait_send()


def lay_out(coarse_ref, *refs):
    inbox, (bands_ref, received_ref) = refs[:len(PARTS)], refs[len(PARTS):]
    bands_ref[...] = coarse_ref[...]

    def unpack(k, carry):
        rows = pl.ds(pl.multiple_of(8 * k, 8), 8)
        for part, (first, count, stride) in enumerate(PARTS):
            for x in range(count):
                at = (first + stride * x) * 128
                received_ref[rows, at:at + 128] = inbox[part][pl.ds(8 * k * count + x, 8, count), :]
        return carry

    lax.fori_loop(0, received_ref.shape[0] // 8, unpack, 0)


def source_table(writers, groups, capacity):
    count = writers.shape[0]
    place = jnp.arange(count, dtype=jnp.int32)
    same = (writers[:, None] == writers[None, :]) & (place[None, :] < place[:, None])
    targets = writers * capacity + jnp.sum(same.astype(jnp.int32), axis=1)
    slots = jnp.arange(groups * capacity, dtype=jnp.int32)
    hit = (targets[None, :] == slots[:, None]).astype(jnp.int32)
    return count - jnp.sum(hit * (count - place)[None, :], axis=1)


def body(fields, tile_writer):
    n_gx, n_gy, n_gz = lax.axis_size("gx"), lax.axis_size("gy"), lax.axis_size("gz")
    n_f, bz, bx, by = fields.shape
    count = n_f * bz
    groups = n_gx * n_gy
    capacity = max(2, 7 * count // (5 * groups) + 1)
    source = source_table(tile_writer.reshape(count), groups, capacity)
    f32 = jnp.float32
    steps = [1 << level for level in range(LEVELS)]
    tables = constant_tables()
    scratch = [pltpu.VMEM(a.shape, a.dtype) for a in (fields, *tables)]
    scratch += [pltpu.VMEM((count + 1, bx, by), f32), pltpu.VMEM((7, bx, by), f32), pltpu.SemaphoreType.DMA((6,))]
    scratch += [pltpu.VMEM((groups, capacity, p[1], by), f32) for p in PARTS]
    scratch += [pltpu.VMEM((2, n_f, 2 * bz // s, by), f32) for s in steps] * 2
    scratch += [pltpu.VMEM((n_f, bx // s, by), f32) for s in steps]
    scratch += [pltpu.VMEM((2, n_f, bx // s, by), f32) for s in steps]
    scratch += [pltpu.VMEM((2, n_f, 2, bx, by) if s == 1 else (2, n_f, bx // s, by), f32) for s in steps] * 2
    scratch += [pltpu.VMEM((2, bx, by), f32) for s in steps] + [pltpu.VMEM((2, 2, bx, by), f32) for s in steps]
    scratch += [pltpu.VMEM((32, by), f32)] * 2 + [pltpu.VMEM((n_gz, 32, by), f32)]
    scratch += [pltpu.SemaphoreType.DMA((3 * LEVELS, 2, n_f))] * 2
    scratch += [pltpu.SemaphoreType.DMA((LEVELS, 2, 2))] * 2
    scratch += [pltpu.SemaphoreType.DMA((n_gz,))] * 2 + [pltpu.SemaphoreType.DMA((len(PARTS), groups))] * 2
    scratch += [pltpu.SemaphoreType.DMA((len(PARTS),))]
    coarse, *inbox = pl.pallas_call(
        functools.partial(kernel, (n_gx, n_gy, n_gz, n_f, bz, capacity)),
        out_shape=(jax.ShapeDtypeStruct((n_f, 2 * n_gz, 2, by // 8), f32),
                   *[jax.ShapeDtypeStruct((groups * capacity, p[1], by), f32) for p in PARTS]),
        in_specs=[pl.BlockSpec(memory_space=pltpu.SMEM)] + [pl.BlockSpec(memory_space=pltpu.HBM)] * 6,
        out_specs=(pl.BlockSpec(memory_space=pltpu.VMEM), *[pl.BlockSpec(memory_space=pltpu.HBM)] * len(PARTS)),
        scratch_shapes=scratch,
        compiler_params=pltpu.CompilerParams(collective_id=0, has_side_effects=True,
                                             vmem_limit_bytes=60 * 1024 * 1024),
    )(source, fields, *tables)
    rows = groups * capacity
    block = 40 if rows % 40 == 0 else 64
    bands = pl.BlockSpec(coarse.shape, lambda i: (0, 0, 0, 0))
    return pl.pallas_call(
        lay_out,
        grid=(rows // block,),
        out_shape=(jax.ShapeDtypeStruct(coarse.shape, f32), jax.ShapeDtypeStruct((rows, bx * by), f32)),
        in_specs=[bands] + [pl.BlockSpec((block * p[1], by), lambda i: (i, 0)) for p in PARTS],
        out_specs=(bands, pl.BlockSpec((block, bx * by), lambda i: (i, 0))),
        compiler_params=pltpu.CompilerParams(vmem_limit_bytes=60 * 1024 * 1024),
    )(coarse, *[part.reshape(-1, by) for part in inbox])


def solution(mesh):
    return jax.shard_map(
        body,
        mesh=mesh,
        in_specs=(P(None, "gz", "gx", "gy"), P("gx", "gy", "gz", None)),
        out_specs=(P(None, None, "gx", "gy"), P(("gx", "gy"), "gz")),
        check_vma=False,
    )
```

```python
import functools

import jax
import jax.numpy as jnp
import numpy as np
from jax import lax
from jax.experimental import pallas as pl
from jax.experimental.pallas import tpu as pltpu
from jax.sharding import PartitionSpec as P

P1 = -1.586134342059924
U1 = -0.052980118572961
P2 = 0.882911075530934
U2 = 0.443506852043971
LOW = 1.0 / 1.149604398860241
HIGH = 1.149604398860241
LEVELS = 3
PARTS = ((1, 8, 2), (2, 4, 4), (0, 4, 4))


def lift_matrix(n, step):
    basis = np.eye(n + 4)
    v, (a, b, c, e) = basis[:n].copy(), basis[n:]
    v[::step] = np.stack(lift_layers(list(v[::step]), a, b, c, e))
    return v


def edge_matrix(n, step):
    below, above = edge_sums(lambda k: np.eye(n)[k * step], n // step)
    return np.stack(below + above)


def tiles_at_once(level):
    return min(8, 16 >> level)


def matrices(level):
    step, t = 1 << level, tiles_at_once(level)
    x_all, x_edge, y_all, y_edge = lift_matrix(16, step), edge_matrix(16, step), lift_matrix(128, step), edge_matrix(128, step)
    mx, hx, ex = np.zeros((128, 128)), np.zeros((128, 32)), np.zeros((32, 128))
    for i in range(t):
        rows = slice(16 * i, 16 * i + 16)
        mx[rows, rows] = x_all[:, :16]
        for way in range(2):
            edge = slice(2 * t * way + 2 * i, 2 * t * way + 2 * i + 2)
            hx[rows, edge] = x_all[:, 16 + 2 * way:18 + 2 * way]
            ex[edge, rows] = x_edge[2 * way:2 * way + 2]
    mq, hy = np.zeros((128, 256)), np.zeros((128, 128))
    mq[:, :128] = y_all[:, :128].T
    for sum_index, offset in enumerate((2, 0, 3, 4)):
        hy[offset * step] = y_all[:, 128 + sum_index]
        for group in range(16):
            mq[:, 128 + group // step * (8 * step) + group % step + offset * step] = y_edge[sum_index]
    return mx, hx, ex, mq, hy


def constant_tables():
    tables = []
    for kind in zip(*[matrices(level) for level in range(LEVELS)]):
        whole = np.stack(kind).astype(np.float32)
        high = whole.astype(jnp.bfloat16)
        low = (whole - high.astype(np.float32)).astype(jnp.bfloat16)
        tables.append(jnp.asarray(np.stack([high, low], axis=1)))
    return tables


def halves(v):
    high = v.astype(jnp.bfloat16)
    return high, (v - high.astype(jnp.float32)).astype(jnp.bfloat16)


def product(a, b):
    dot = lambda p, q: jnp.dot(p, q, preferred_element_type=jnp.float32)
    return dot(a[0], b[0]) + dot(a[1], b[0]) + dot(a[0], b[1])


def edge_sums(get, n):
    a = get(n - 1) + P1 * get(n - 2)
    before = get(n - 3) + P1 * (get(n - 4) + get(n - 2))
    b = get(n - 2) + U1 * before
    c = get(0)
    after = get(1) + P1 * (c + get(2))
    e = c + U1 * after
    return (a, b), (c, e)


def lift_layers(v, a, b, c, e):
    s, d = list(v[0::2]), list(v[1::2])
    n = len(s)
    s_end = [c]
    d = [d[i] + P1 * (s[i] + (s + s_end)[i + 1]) for i in range(n)]
    dm = a + P1 * s[0]
    sm = b + U1 * dm
    s_top = e + U1 * d[-1]
    s = [s[i] + U1 * (([dm] + d)[i] + d[i]) for i in range(n)]
    d = [d[i] + P2 * (s[i] + (s + [s_top])[i + 1]) for i in range(n)]
    dm = dm + P2 * (sm + s[0])
    s = [s[i] + U2 * (([dm] + d)[i] + d[i]) for i in range(n)]
    out = []
    for i in range(n):
        out += [s[i] * LOW, d[i] * HIGH]
    return out


def lift_whole(v):
    s, d = list(v[0::2]), list(v[1::2])
    n = len(s)
    d = [d[i] + P1 * (s[i] + s[(i + 1) % n]) for i in range(n)]
    s = [s[i] + U1 * (d[i - 1] + d[i]) for i in range(n)]
    d = [d[i] + P2 * (s[i] + s[(i + 1) % n]) for i in range(n)]
    s = [s[i] + U2 * (d[i - 1] + d[i]) for i in range(n)]
    out = []
    for i in range(n):
        out += [s[i] * LOW, d[i] * HIGH]
    return out


def kernel(sizes, source_ref, *refs):
    n_gx, n_gy, n_gz, n_f, bz, capacity = sizes
    given, coarse_ref, inbox, held, scratch = refs[:6], refs[6], refs[7:10], refs[10:16], refs[16:]
    fields_ref, mx_ref, hx_ref, ex_ref, mq_ref, hy_ref = held
    work, turn_rows, load_sem = scratch[:3]
    outbox, scratch = scratch[3:6], scratch[6:]
    loads = [pltpu.make_async_copy(a, b, load_sem.at[i]) for i, (a, b) in enumerate(zip(given, held))]
    for load in loads:
        load.start()
    xs, xr, ys, yr, zs, zr, cs, cr = [scratch[LEVELS * i:LEVELS * (i + 1)] for i in range(8)]
    low_rows, gs, gr, send, recv, c_send, c_recv, g_send, g_recv, a_send, a_recv, own_sem = scratch[8 * LEVELS:]
    groups = n_gx * n_gy
    ix, iy, iz = lax.axis_index("gx"), lax.axis_index("gy"), lax.axis_index("gz")
    me = ix * n_gy + iy
    place = {"gx": (ix, n_gx), "gy": (iy, n_gy), "gz": (iz, n_gz)}
    MESH = pl.DeviceIdType.MESH

    def beside(axis, way):
        index, count = place[axis]
        return lax.rem(index + (1 if way == 0 else count - 1), count)

    barrier = pltpu.get_barrier_semaphore()

    def greet_plane(k, carry):
        w = lax.rem(me + k, groups)
        pl.semaphore_signal(barrier, inc=1, device_id={"gx": w // n_gy, "gy": lax.rem(w, n_gy)},
                            device_id_type=MESH)
        return carry

    lax.fori_loop(1, groups, greet_plane, 0)
    for k in range(1, n_gz):
        pl.semaphore_signal(barrier, inc=1, device_id={"gz": lax.rem(iz + k, n_gz)}, device_id_type=MESH)
    for yway in range(2):
        for zway in range(2):
            pl.semaphore_signal(barrier, inc=1, device_id={"gy": beside("gy", yway), "gz": beside("gz", zway)},
                                device_id_type=MESH)
    for load in loads:
        load.wait()
    pl.semaphore_wait(barrier, groups - 1 + n_gz - 1 + 4)

    def exchange(level, kind, f, way):
        axis = ("gx", "gy", "gz")[kind]
        out, into = ((xs, xr), (ys, yr), (zs, zr))[kind]
        src = out[level] if kind == 1 else out[level].at[way]
        dst = into[level].at[way]
        if level < 2:
            src, dst = src.at[f], dst.at[f]
        row = level * 3 + kind
        return pltpu.make_async_remote_copy(
            src_ref=src, dst_ref=dst,
            send_sem=send.at[row, way, f], recv_sem=recv.at[row, way, f],
            device_id={axis: beside(axis, way)}, device_id_type=MESH)

    def corner(level, yway, zway):
        return pltpu.make_async_remote_copy(
            src_ref=cs[level].at[zway], dst_ref=cr[level].at[yway, zway],
            send_sem=c_send.at[level, yway, zway], recv_sem=c_recv.at[level, yway, zway],
            device_id={"gy": beside("gy", yway), "gz": beside("gz", zway)}, device_id_type=MESH)

    row = lax.broadcasted_iota(jnp.int32, (16, 128), 0)
    lane = lax.broadcasted_iota(jnp.int32, (16, 128), 1)

    def send_x(level, f, tiles):
        t = tiles_at_once(level)
        sums = tuple(ex_ref[level, half, :4 * t, :16 * t] for half in range(2))
        for k in range(0, len(tiles), t):
            edge = product(sums, halves(jnp.concatenate(tiles[k:k + t], axis=0)))
            for way in range(2):
                    xs[level][way, f, 2 * k:2 * (k + t), :] = edge[2 * t * way:2 * t * (way + 1)]
        if level < 2:
            per_field(level, f, start, [0])

    def spot(i, step):
        return i // step * (8 * step) + i % step

    def packed(step, pairs, pack):
        for i, v in pairs:
            start = i // step * (8 * step)
            here = (lane >= start) & (lane < start + 8 * step) & (lane % step == i % step)
            pack = jnp.where(here, v, pack)
        return pack

    def edge_lanes(step, below, above, spots):
        both = jnp.where(lane % (8 * step) // step < 3, below, above)
        return [pltpu.roll(both, (128 - spot(i, step)) % 128, 1) for i in spots]

    def planes(f, step, ref):
        return [ref[f * bz + z] if ref is work else ref[f, z] for z in range(0, bz, step)]

    def put(f, step, tiles):
        for i, tile in enumerate(tiles):
            work[f * bz + i * step] = tile

    def per_field(level, f, act, kinds):
        if level < 2 or (isinstance(f, int) and f == 0):
            for kind in kinds:
                for way in range(2):
                    act(exchange(level, kind, f, way))

    def start(copy):
        copy.start()

    def arrive(copy):
        copy.wait_recv()

    def stage(level, body):
        if level < 2:
            loop(body)
        else:
            for f in range(n_f):
                body(f)

    def loop(body):
        def run(f, carry):
            body(f)
            return carry
        lax.fori_loop(0, n_f, run, 0)

    def squeeze(slot, v, step):
        if step == 1:
            return v
        turn_rows[slot] = v
        return turn_rows[slot, pl.ds(0, 16 // step, step), :]

    def spread(slot, v, step):
        if step == 1:
            return v
        turn_rows[slot, pl.ds(0, 16 // step, step), :] = v
        return turn_rows[slot]

    def route(part, k):
        w = lax.rem(me + k, groups)
        return pltpu.make_async_remote_copy(
            src_ref=outbox[part].at[w], dst_ref=inbox[part].at[pl.ds(me * capacity, capacity)],
            send_sem=a_send.at[part, k], recv_sem=a_recv.at[part, k],
            device_id={"gx": w // n_gy, "gy": lax.rem(w, n_gy)}, device_id_type=MESH)

    def own(part):
        return pltpu.make_async_copy(
            outbox[part].at[me], inbox[part].at[pl.ds(me * capacity, capacity)], own_sem.at[part])

    def fill(part, w):
        first, count, stride = PARTS[part]
        for r in range(capacity):
            outbox[part][w, r] = work[source_ref[w * capacity + r], pl.ds(first, count, stride), :]

    def ship(part, first, last):
        def run(k, carry):
            fill(part, lax.rem(me + k, groups))
            route(part, k).start()
            return carry
        lax.fori_loop(first, last, run, 0)

    cuts = [1 + (groups - 1) * i // 2 for i in range(3)]
    turn_rows[...] = jnp.zeros_like(turn_rows)
    work[n_f * bz] = jnp.zeros((16, 128), jnp.float32)
    loop(lambda f: send_x(0, f, planes(f, 1, fields_ref)))
    for level in range(LEVELS):
        step = 1 << level
        if level > 0:
            ship(level - 1, cuts[0], cuts[1])
        for zway in range(2):
            cs[level][zway] = jnp.zeros((16, 128), jnp.float32)

        t = tiles_at_once(level)
        live = (row % step == 0) & (lane % step == 0)

        def x_stage(f, level=level, step=step, t=t, live=live):
            tiles = planes(f, step, fields_ref if level == 0 else work)
            per_field(level, f, arrive, [0])
            mx = tuple(mx_ref[level, half, :16 * t, :16 * t] for half in range(2))
            hx = tuple(hx_ref[level, half, :16 * t, :4 * t] for half in range(2))
            mq = tuple(mq_ref[level, half] for half in range(2))
            wide = []
            for k in range(0, len(tiles), t):
                edge = jnp.concatenate([xr[level][way, f, 2 * k:2 * (k + t), :] for way in range(2)], axis=0)
                lifted = product(mx, halves(jnp.concatenate(tiles[k:k + t], axis=0))) + product(hx, halves(edge))
                lifted = product(halves(lifted), mq)
                wide += [lifted[16 * i:16 * i + 16] for i in range(t)]
            own_lanes, sum_lanes = [w[:, :128] for w in wide], [w[:, 128:] for w in wide]
            put(f, step, own_lanes if step == 1 else [jnp.where(live, n, o) for n, o in zip(own_lanes, tiles)])
            sums = edge_sums(lambda k: own_lanes[k], len(wide))
            for way in range(2):
                if step == 1:
                    for j in range(2):
                        zs[level][way, f, j] = sums[way][j]
                else:
                    mixed = jnp.where(lane % step == 0, sums[way][0], pltpu.roll(sums[way][1], 1, 1))
                    zs[level][way, f] = squeeze(way, mixed, step)
            if level < 2:
                per_field(level, f, start, [2])
            pack = packed(step, list(enumerate(sum_lanes)), jnp.zeros((16, 128), jnp.float32))
            ys[level][f] = squeeze(2, pack, step)
            if level < 2:
                per_field(level, f, start, [1])
            sums = edge_sums(lambda k: sum_lanes[k], len(wide))
            for way in range(2):
                cs[level][way] = packed(step, [(2 * f + j, sums[way][j]) for j in range(2)], cs[level][way])

        stage(level, x_stage)
        if level == 2:
            per_field(level, 0, start, [2, 1])
        for yway in range(2):
            for zway in range(2):
                corner(level, yway, zway).start()
        if level > 0:
            ship(level - 1, cuts[1], cuts[2])
            fill(level - 1, me)
            own(level - 1).start()

        for yway in range(2):
            for zway in range(2):
                corner(level, yway, zway).wait_recv()

        def z_stage(f, level=level, step=step, live=live):
            old = planes(f, step, work)
            per_field(level, f, arrive, [1, 2])
            hy = tuple(hy_ref[level, half] for half in range(2))
            edges = edge_lanes(step, spread(3, yr[level][0, f], step), spread(4, yr[level][1, f], step), range(len(old)))
            for way in range(2):
                edges += edge_lanes(step, cr[level][0, way], cr[level][1, way], [2 * f, 2 * f + 1])
            extra = product(halves(jnp.concatenate(edges, axis=0)), hy)
            if step > 1:
                extra = jnp.where((lax.broadcasted_iota(jnp.int32, extra.shape, 0) % step) == 0, extra, 0.0)
            extra = [extra[16 * i:16 * i + 16] for i in range(len(edges))]
            far = []
            for way in range(2):
                if step == 1:
                    far += [zr[level][way, f, 0], zr[level][way, f, 1]]
                else:
                    mixed = spread(5 + way, zr[level][way, f], step)
                    far += [mixed, pltpu.roll(mixed, 127, 1)]
            edge = [v + x for v, x in zip(far, extra[len(old):])]
            old = [o + x for o, x in zip(old, extra)]
            new = lift_layers(old, *edge)
            if step > 1:
                new = [jnp.where(live, n, o) for n, o in zip(new, old)]
            put(f, step, new)
            if level + 1 < LEVELS:
                send_x(level + 1, f, new[::2])

        stage(level, z_stage)
        if level == 1:
            per_field(2, 0, start, [0])

    def gather(k):
        return pltpu.make_async_remote_copy(
            src_ref=gs, dst_ref=gr.at[iz], send_sem=g_send.at[k], recv_sem=g_recv.at[k],
            device_id={"gz": lax.rem(iz + k, n_gz)}, device_id_type=MESH)

    for i in range(2):
        for f in range(n_f):
            for j in range(2):
                low_rows[16 * i + 2 * f + j:16 * i + 2 * f + j + 1, :] = work[f * bz + 8 * i, 8 * j:8 * j + 1, :]
        low_rows[16 * i + 2 * n_f:16 * i + 16, :] = jnp.zeros((16 - 2 * n_f, 128), jnp.float32)
    pick = jnp.where(lax.broadcasted_iota(jnp.int32, (128, 128), 0) ==
                     8 * lax.broadcasted_iota(jnp.int32, (128, 128), 1), jnp.float32(1.0), jnp.float32(0.0))
    gs[...] = jnp.dot(low_rows[...], pick, precision=lax.Precision.HIGHEST, preferred_element_type=jnp.float32)
    for k in range(1, n_gz):
        gather(k).start()
    gr[iz] = gs[...]

    last = len(PARTS) - 1
    ship(last, 1, groups)
    fill(last, me)
    own(last).start()

    for k in range(1, n_gz):
        gather(k).wait_recv()
    four = lift_whole([gr[g, 16 * i:16 * i + 16, :] for g in range(n_gz) for i in range(2)])
    four[::2] = lift_whole(four[::2])
    for z, tile in enumerate(four):
        for f in range(n_f):
            coarse_ref[f, z] = tile[2 * f:2 * f + 2, :16]

    def finish(k, carry):
        for part in range(len(PARTS)):
            route(part, k).wait()
        return carry

    lax.fori_loop(1, groups, finish, 0)
    for part in range(len(PARTS)):
        own(part).wait()

    for k in range(1, n_gz):
        gather(k).wait_send()

    def sent(f):
        for level in range(2):
            for kind in range(3):
                for way in range(2):
                    exchange(level, kind, f, way).wait_send()

    loop(sent)
    per_field(2, 0, lambda copy: copy.wait_send(), range(3))
    for level in range(LEVELS):
        for yway in range(2):
            for zway in range(2):
                corner(level, yway, zway).wait_send()


def lay_out(coarse_ref, *refs):
    inbox, (bands_ref, received_ref) = refs[:len(PARTS)], refs[len(PARTS):]
    bands_ref[...] = coarse_ref[...]

    def unpack(k, carry):
        rows = pl.ds(pl.multiple_of(8 * k, 8), 8)
        for part, (first, count, stride) in enumerate(PARTS):
            for x in range(count):
                at = (first + stride * x) * 128
                received_ref[rows, at:at + 128] = inbox[part][pl.ds(8 * k * count + x, 8, count), :]
        return carry

    lax.fori_loop(0, received_ref.shape[0] // 8, unpack, 0)


def source_table(writers, groups, capacity):
    count = writers.shape[0]
    place = jnp.arange(count, dtype=jnp.int32)
    same = (writers[:, None] == writers[None, :]) & (place[None, :] < place[:, None])
    targets = writers * capacity + jnp.sum(same.astype(jnp.int32), axis=1)
    slots = jnp.arange(groups * capacity, dtype=jnp.int32)
    hit = (targets[None, :] == slots[:, None]).astype(jnp.int32)
    return count - jnp.sum(hit * (count - place)[None, :], axis=1)


def body(fields, tile_writer):
    n_gx, n_gy, n_gz = lax.axis_size("gx"), lax.axis_size("gy"), lax.axis_size("gz")
    n_f, bz, bx, by = fields.shape
    count = n_f * bz
    groups = n_gx * n_gy
    capacity = max(2, 7 * count // (5 * groups) + 1)
    source = source_table(tile_writer.reshape(count), groups, capacity)
    f32 = jnp.float32
    steps = [1 << level for level in range(LEVELS)]
    tables = constant_tables()
    scratch = [pltpu.VMEM(a.shape, a.dtype) for a in (fields, *tables)]
    scratch += [pltpu.VMEM((count + 1, bx, by), f32), pltpu.VMEM((7, bx, by), f32), pltpu.SemaphoreType.DMA((6,))]
    scratch += [pltpu.VMEM((groups, capacity, p[1], by), f32) for p in PARTS]
    scratch += [pltpu.VMEM((2, n_f, 2 * bz // s, by), f32) for s in steps] * 2
    scratch += [pltpu.VMEM((n_f, bx // s, by), f32) for s in steps]
    scratch += [pltpu.VMEM((2, n_f, bx // s, by), f32) for s in steps]
    scratch += [pltpu.VMEM((2, n_f, 2, bx, by) if s == 1 else (2, n_f, bx // s, by), f32) for s in steps] * 2
    scratch += [pltpu.VMEM((2, bx, by), f32) for s in steps] + [pltpu.VMEM((2, 2, bx, by), f32) for s in steps]
    scratch += [pltpu.VMEM((32, by), f32)] * 2 + [pltpu.VMEM((n_gz, 32, by), f32)]
    scratch += [pltpu.SemaphoreType.DMA((3 * LEVELS, 2, n_f))] * 2
    scratch += [pltpu.SemaphoreType.DMA((LEVELS, 2, 2))] * 2
    scratch += [pltpu.SemaphoreType.DMA((n_gz,))] * 2 + [pltpu.SemaphoreType.DMA((len(PARTS), groups))] * 2
    scratch += [pltpu.SemaphoreType.DMA((len(PARTS),))]
    coarse, *inbox = pl.pallas_call(
        functools.partial(kernel, (n_gx, n_gy, n_gz, n_f, bz, capacity)),
        out_shape=(jax.ShapeDtypeStruct((n_f, 2 * n_gz, 2, by // 8), f32),
                   *[jax.ShapeDtypeStruct((groups * capacity, p[1], by), f32) for p in PARTS]),
        in_specs=[pl.BlockSpec(memory_space=pltpu.SMEM)] + [pl.BlockSpec(memory_space=pltpu.HBM)] * 6,
        out_specs=(pl.BlockSpec(memory_space=pltpu.VMEM), *[pl.BlockSpec(memory_space=pltpu.HBM)] * len(PARTS)),
        scratch_shapes=scratch,
        compiler_params=pltpu.CompilerParams(collective_id=0, has_side_effects=True,
                                             vmem_limit_bytes=60 * 1024 * 1024),
    )(source, fields, *tables)
    rows = groups * capacity
    block = 40 if rows % 40 == 0 else 64
    bands = pl.BlockSpec(coarse.shape, lambda i: (0, 0, 0, 0))
    return pl.pallas_call(
        lay_out,
        grid=(rows // block,),
        out_shape=(jax.ShapeDtypeStruct(coarse.shape, f32), jax.ShapeDtypeStruct((rows, bx * by), f32)),
        in_specs=[bands] + [pl.BlockSpec((block * p[1], by), lambda i: (i, 0)) for p in PARTS],
        out_specs=(bands, pl.BlockSpec((block, bx * by), lambda i: (i, 0))),
        compiler_params=pltpu.CompilerParams(vmem_limit_bytes=60 * 1024 * 1024),
    )(coarse, *[part.reshape(-1, by) for part in inbox])


def solution(mesh):
    return jax.shard_map(
        body,
        mesh=mesh,
        in_specs=(P(None, "gz", "gx", "gy"), P("gx", "gy", "gz", None)),
        out_specs=(P(None, None, "gx", "gy"), P(("gx", "gy"), "gz")),
        check_vma=False,
    )
```
